512 devices in a mesh: lat: 64 (over x, y, z_hi, core), lon: 8 (over z_lo).
Axes of the slice: x: 4, y: 4, z: 16 (z_hi: 2, z_lo: 8; z = z_hi * 8 + z_lo), core: 2. Of those that a mesh axis runs over, the one named last changes fastest.
Arguments:
- field: bfloat16 [128, 1440, 384], P('lat', 'lon'), may hold values from -6 to 6
- row_shift: int32 [128], P('lat'), may hold values from -1 to 1
- output_tile_index: int32 [128], P('lat'), may hold values from 0 to 15
- tiles: bfloat16 [3, 16, 3, 33], replicated, may hold values from -0.625 to 0.625
- mix: bfloat16 [3, 4, 96, 96], replicated, may hold values from -0.375 to 0.375
- w_in: bfloat16 [384, 768], replicated, may hold values from -0.3125 to 0.3125
- w_out: bfloat16 [768, 384], replicated, may hold values from -0.21875 to 0.21875
- cotangent: bfloat16 [128, 1440, 384], P('lat', 'lon'), may hold values from -6 to 6
Outputs:
- output: bfloat16 [128, 1440, 384], P('lat', 'lon')
- grad_field: bfloat16 [128, 1440, 384], P('lat', 'lon')
- grad_mix: bfloat16 [3, 4, 96, 96], replicated
- grad_in: bfloat16 [384, 768], replicated
- grad_out: bfloat16 [768, 384], replicated
The draws below stay inside these ranges and needn't reach their ends.
All inputs are finite; a program needn't handle non-finite values.
Results may differ from the reference program's by a relative error of at most 0.0069.
Values may be sent and summed in bfloat16 or wider, within the bound.
A program may use at most 64 MiB of HBM per device.

```python
import jax
import jax.numpy as jnp
from jax import lax

D = 384
HID = 768
G = 4
DG = 96
K = 3
NTILE = 16
HB = 1
REACH = 2
WH = 16
WTAP = 33
NLON = 1440
NLAT = 128


def place_ends(values, key, least, top_value):
    dims = values.shape
    spot = [jax.random.randint(jax.random.fold_in(key, axis), (), 0, dims[axis]) for axis in range(len(dims))]
    values = values.at[tuple(spot)].set(least)
    longest = dims.index(max(dims))
    spot[longest] = (spot[longest] + 1) % dims[longest]
    return values.at[tuple(spot)].set(top_value)


def steps_of(own_key, dims, split, smallest, high):
    def one(axis_at, shards_of):
        heights = jax.random.uniform(jax.random.fold_in(jax.random.fold_in(own_key, 6), axis_at), (shards_of,), jnp.float32, smallest / len(split), high / len(split))
        return jnp.repeat(jnp.exp(heights), dims[axis_at] // shards_of).reshape((-1,) + (1,) * (len(dims) - axis_at - 1))

    loudness = one(*split[0])
    for cut in split[1:]:
        loudness = loudness * one(*cut)
    return loudness


def normal_values(stream_key, dims, scale, most, pieces=(), kind=jnp.bfloat16):
    loudness = steps_of(stream_key, dims, pieces, -0.22, 0.18) if pieces else 1.0
    drawn = jax.random.normal(stream_key, dims, jnp.float32) * scale * loudness
    return jnp.minimum(jnp.maximum(drawn, -most), most).astype(kind)


def setup_inputs(seed: int = 0) -> dict:
    keys = jax.random.split(jax.random.key(seed), 9)
    field = normal_values(keys[0], (NLAT, NLON, D), 1.0, 6.0, ((0, 64), (1, 8)))
    row_shift = place_ends(jax.random.randint(keys[1], (NLAT,), -1, 2), jax.random.fold_in(keys[1], 1), -1, 1).astype(jnp.int32)
    output_tile_index = place_ends(jax.random.randint(keys[2], (NLAT,), 0, NTILE), jax.random.fold_in(keys[2], 1), 0, NTILE - 1).astype(jnp.int32)
    tiles = normal_values(keys[3], (K, NTILE, 2 * HB + 1, WTAP), ((2 * HB + 1) * WTAP) ** -0.5, 0.625)
    mix = normal_values(keys[4], (K, G, DG, DG), (K * DG) ** -0.5, 0.375)
    w_in = normal_values(keys[5], (D, HID), D ** -0.5, 0.3125)
    w_out = normal_values(keys[6], (HID, D), HID ** -0.5, 0.21875)
    cotangent = normal_values(keys[7], (NLAT, NLON, D), 1.0, 6.0, ((0, 64), (1, 8)))
    return {"field": field, "row_shift": row_shift, "output_tile_index": output_tile_index, "tiles": tiles, "mix": mix, "w_in": w_in, "w_out": w_out, "cotangent": cotangent}


def reference(field, row_shift, output_tile_index, tiles, mix, w_in, w_out, cotangent):
    width = NLON + 2 * WH
    strip_row_extent = 2 * HB + 1
    hi = lax.Precision.HIGHEST
    taps = jnp.moveaxis(jnp.take(tiles, output_tile_index, axis=1).astype(jnp.float32), 1, 0)
    padded = jnp.pad(field.astype(jnp.float32), ((REACH, REACH), (0, 0), (0, 0)))
    padded = jnp.concatenate([padded[:, NLON - WH:], padded, padded[:, :WH]], axis=1)
    starts = (jnp.arange(NLAT, dtype=jnp.int32) + row_shift.astype(jnp.int32) - HB + REACH).astype(jnp.int32)

    def one_row(item):
        start, kernel_row_offsets = item
        band = lax.dynamic_slice_in_dim(padded, start, strip_row_extent, 0)

        def step(shift, total):
            window = lax.dynamic_slice_in_dim(band, shift, NLON, 1)
            weights = lax.dynamic_slice_in_dim(kernel_row_offsets, shift, 1, 2)[:, :, 0]
            return total + jnp.einsum('bk,kjc->bjc', weights, window, precision=hi)
        return lax.fori_loop(0, WTAP, step, jnp.zeros((K, NLON, D), jnp.float32))
    basis = lax.map(one_row, (starts, taps)).astype(jnp.bfloat16)
    grouped = basis.astype(jnp.float32).reshape(NLAT, K, NLON, G, DG)
    mixf = mix.astype(jnp.float32)
    conv = jnp.einsum('ibjgf,bgfe->ijge', grouped, mixf, precision=hi).reshape(NLAT, NLON, D)
    mixed = (field.astype(jnp.float32) + conv).astype(jnp.bfloat16)
    flat = mixed.reshape(-1, D)
    pre = jnp.dot(flat, w_in, preferred_element_type=jnp.float32)
    hidden = jax.nn.gelu(pre).astype(jnp.bfloat16)
    output = (flat.astype(jnp.float32) + jnp.dot(hidden, w_out, preferred_element_type=jnp.float32)).astype(jnp.bfloat16)
    grad_flat = cotangent.reshape(-1, D)
    grad_hidden = jnp.dot(grad_flat, w_out.T, preferred_element_type=jnp.float32)
    unused, gelu_back = jax.vjp(jax.nn.gelu, pre)
    grad_pre = gelu_back(grad_hidden)[0].astype(jnp.bfloat16)
    grad_mixed = (grad_flat.astype(jnp.float32) + jnp.dot(grad_pre, w_in.T, preferred_element_type=jnp.float32)).astype(jnp.bfloat16)
    grad_in = jnp.dot(flat.T, grad_pre, preferred_element_type=jnp.float32).astype(jnp.bfloat16)
    grad_out = jnp.dot(hidden.T, grad_flat, preferred_element_type=jnp.float32).astype(jnp.bfloat16)
    grad_grouped = grad_mixed.astype(jnp.float32).reshape(NLAT, NLON, G, DG)
    grad_mix = jnp.einsum('ibjgf,ijge->bgfe', grouped, grad_grouped, precision=hi).astype(jnp.bfloat16)
    filter_basis_gradient = jnp.einsum('ijge,bgfe->ibjgf', grad_grouped, mixf, precision=hi).reshape(NLAT, K, NLON, D).astype(jnp.bfloat16)

    def back_row(carry, item):
        start, kernel_row_offsets, grad_row = item
        gradf = grad_row.astype(jnp.float32)

        def step(shift, band):
            weights = lax.dynamic_slice_in_dim(kernel_row_offsets, shift, 1, 2)[:, :, 0]
            piece = jnp.einsum('bk,bjc->kjc', weights, gradf, precision=hi)
            current = lax.dynamic_slice_in_dim(band, shift, NLON, 1)
            return lax.dynamic_update_slice_in_dim(band, current + piece, shift, 1)
        band = lax.fori_loop(0, WTAP, step, jnp.zeros((strip_row_extent, width, D), jnp.float32))
        old = lax.dynamic_slice_in_dim(carry, start, strip_row_extent, 0)
        return (lax.dynamic_update_slice_in_dim(carry, old + band, start, 0), None)
    grad_padded, unused_rows = lax.scan(back_row, jnp.zeros((NLAT + 2 * REACH, width, D), jnp.float32), (starts, taps, filter_basis_gradient))
    core = grad_padded[:, WH:WH + NLON]
    core = core.at[:, NLON - WH:].add(grad_padded[:, :WH])
    core = core.at[:, :WH].add(grad_padded[:, WH + NLON:])
    grad_conv = core[REACH:REACH + NLAT]
    grad_field = (grad_mixed.astype(jnp.float32).reshape(NLAT, NLON, D) + grad_conv).astype(jnp.bfloat16)
    return (output.reshape(NLAT, NLON, D), grad_field, grad_mix, grad_in, grad_out)
```

```python
import functools

import jax
import jax.numpy as jnp
from jax import lax
from jax.experimental import pallas as pl
from jax.experimental.pallas import tpu as pltpu
from jax.sharding import PartitionSpec as P

D = 384
HID = 768
G = 4
DG = 96
K = 3
WTAP = 33
NLAT = 128
WH = 16
ROWS = 2
LON = 180
PAD = 192
JB = 64
NJ = 3
WIN = 128
EXT = 256
OFF = 5
CELLS = ROWS * PAD
TILES = 384
HALF = TILES // 2
PER = HALF // 16
MESH = pl.DeviceIdType.MESH
F32 = jnp.float32
BF16 = jnp.bfloat16


def dot(a, b, contract=((1,), (0,))):
    return lax.dot_general(a, b, (contract, ((), ())), preferred_element_type=F32)


def position():
    lat, lon = lax.axis_index("lat"), lax.axis_index("lon")
    return lat // 16, (lat // 4) % 4, ((lat // 2) % 2) * 8 + lon, lat % 2


def device(x, y, z, core):
    return (((x * 4 + y) * 2 + z // 8) * 2 + core, z % 8)


def remote(src, dst, send_sem, recv_sem, to):
    return pltpu.make_async_remote_copy(
        src_ref=src, dst_ref=dst, send_sem=send_sem, recv_sem=recv_sem, device_id=to, device_id_type=MESH
    )


class Halo:
    def __init__(self, sems_out, sems_in):
        lat, lon = lax.axis_index("lat"), lax.axis_index("lon")
        x, y, z, core = position()
        self.core = core
        step = 1 - 2 * core
        self.near = (lat + step, lon)
        self.far = ((lat + 64 - step) % 64, lon)
        west, east = (lon + 7) % 8, (lon + 1) % 8
        self.west, self.east = (lat, west), (lat, east)
        self.near_west, self.near_east = (lat + step, west), (lat + step, east)
        self.far_west, self.far_east = (self.far[0], west), (self.far[0], east)
        towards = 4 * (2 * core - 1)
        self.relay = device(x, y, (z + towards + 16) % 16, core)
        source_z = (z - towards + 16) % 16
        source = device(x, y, source_z, core)
        self.source = source
        self.beyond = ((source[0] + 64 - step) % 64, source[1])
        far_lat = self.far[0]
        self.passer = device(far_lat // 16, (far_lat // 4) % 4, (z + 8 - towards + 16) % 16, 1 - core)
        self.sems_out, self.sems_in = sems_out, sems_in

    def copy(self, i, src, dst, to):
        return remote(src, dst, self.sems_out.at[i], self.sems_in.at[i], to)


def kernel(
    shift_ref, index_ref, field_ref, cot_ref, tiles_ref, mix_ref, win_ref, wout_ref,
    out_ref, gfield_ref, gmix_ref, gin_ref, gout_ref,
    ext, east_in, east_out, relay, cot, taps, strip, mixd, basis, mixed, hidden, gpre, ghid, pre,
    gmixed, gbasis, gext, rim_out, rim_relay, rim_near, rim_far, side_out, side_in,
    part, core_in, half_out, plane_in, z_out, z_in, z_all, total,
    halo_s, halo_r, rim_s, rim_r, core_s, core_r, plane_s, plane_r, z_s, z_r, zg_s, zg_r, pg_s, pg_r, cg_s, cg_r,
):
    x, y, z, core = position()
    lat, lon = lax.axis_index("lat"), lax.axis_index("lon")
    halo = Halo(halo_s, halo_r)
    other = device(x, y, z, 1 - core)

    def plane_peer(k):
        px, py = (x + k // 4) % 4, (y + k % 4) % 4
        return px * 4 + py, device(px, py, z, core)

    def z_peer(k):
        pz = (z + k) % 16
        return pz, device(x, y, pz, core)

    barrier = pltpu.get_barrier_semaphore()
    greet = [halo.near, halo.far, halo.west, halo.east, halo.near_west, halo.near_east, halo.far_west, halo.far_east]
    greet += [halo.relay, halo.source, halo.beyond, halo.passer]
    greet += [plane_peer(k)[1] for k in range(1, 16)] + [z_peer(k)[1] for k in range(1, 16)]
    for to in greet:
        pl.semaphore_signal(barrier, inc=1, device_id=to, device_id_type=MESH)

    ext[2:4, PAD:EXT] = jnp.zeros((2, EXT - PAD, D), BF16)
    for r in (0, 1, 4, 5):
        ext[r, WH + PAD:EXT] = jnp.zeros((EXT - WH - PAD, D), BF16)
    for r in range(ROWS):
        ext[2 + r, WH:WH + LON] = field_ref[r]
        cot[r, PAD - 16:PAD] = jnp.zeros((16, D), BF16)
        cot[r, 0:LON] = cot_ref[r]
        edge = ext[2 + r, 176:208].astype(F32)
        east_out[r] = pltpu.roll(edge, 28, 0)[:WH].astype(BF16)

    pl.semaphore_wait(barrier, len(greet))

    near_at = core * 4
    far_at = 4 - core * 4
    sends = []
    for k in range(NJ):
        sends.append(halo.copy(k, ext.at[2:4, pl.ds(WH + JB * k, JB)], relay.at[:, pl.ds(JB * k, JB)], halo.relay))
    own_west = ext.at[2:4, 16:32]
    corners = [
        halo.copy(7, own_west, east_in.at[pl.ds(far_at, 2)], halo.far_west),
        halo.copy(8, east_out, ext.at[pl.ds(far_at, 2), 0:16], halo.far_east),
        halo.copy(9, own_west, east_in.at[2:4], halo.west),
        halo.copy(10, east_out, ext.at[2:4, 0:16], halo.east),
        halo.copy(11, own_west, east_in.at[pl.ds(near_at, 2)], halo.near_west),
        halo.copy(12, east_out, ext.at[pl.ds(near_at, 2), 0:16], halo.near_east),
    ]
    near = halo.copy(6, ext.at[2:4, WH:WH + PAD], ext.at[pl.ds(near_at, 2), WH:WH + PAD], halo.near)
    for c in sends + corners + [near]:
        c.start()

    ghid[...] = dot(cot[...].reshape(CELLS, D), wout_ref[...], ((1,), (1,)))
    group = lambda n: (n >= DG).astype(jnp.int32) + (n >= 2 * DG).astype(jnp.int32) + (n >= 3 * DG).astype(jnp.int32)
    row_i, col_i = (lax.broadcasted_iota(jnp.int32, (D, D), d) for d in (0, 1))
    block = group(row_i) == group(col_i)
    s_row, s_col = (lax.broadcasted_iota(jnp.int32, (DG, D), d) for d in (0, 1))
    spread = (s_row == s_col - DG * group(s_col)).astype(BF16)
    for b in range(K):
        wide = dot(mix_ref[b].reshape(D, DG), spread)
        mixd[D * b:D * b + D] = jnp.where(block, wide, 0.0).astype(BF16)
    taps[...] = jnp.zeros((32, 128), F32)
    for r in range(ROWS):
        s, t = shift_ref[r], index_ref[r]
        for b in range(K):
            tile = tiles_ref[b, t].astype(F32)
            for o in range(OFF):
                line = jnp.zeros((1, WTAP), F32)
                here = lat * ROWS + r + o - 2
                inside = jnp.logical_and(here >= 0, here < NLAT)
                for k in range(K):
                    line = jnp.where(jnp.logical_and(inside, k == o - 1 - s), tile[k:k + 1], line)
                n = (r * K + b) * OFF + o
                taps[n:n + 1, 0:WTAP] = line
    for r in range(ROWS):
        for b in range(K):
            for o in range(OFF):
                n = (r * K + b) * OFF + o
                line = jnp.broadcast_to(taps[n:n + 1], (JB, WIN))
                strip[r, JB * b:JB * b + JB, WIN * o:WIN * o + WIN] = pltpu.roll(
                    line, 0, 1, stride=1, stride_axis=0).astype(BF16)

    for k in range(NJ):
        sends[k].wait_recv()
        c = halo.copy(3 + k, relay.at[:, pl.ds(JB * k, JB)], ext.at[pl.ds(far_at, 2), pl.ds(WH + JB * k, JB)], halo.beyond)
        c.start()
        sends.append(c)

    near.wait_recv()
    for c in corners:
        c.wait_recv()
    for k in range(NJ):
        sends[3 + k].wait_recv()
    for c in sends[:NJ] + [near]:
        c.wait_send()
    for r in range(6):
        edge = jnp.concatenate([east_in[r].astype(F32), jnp.zeros((WH, D), F32)], axis=0)
        ext[r, PAD:PAD + 32] = (ext[r, PAD:PAD + 32].astype(F32) + pltpu.roll(edge, 4, 0)).astype(BF16)

    for r in range(ROWS):
        for j in range(NJ):
            window = ext[r:r + OFF, JB * j:JB * j + WIN].reshape(OFF * WIN, D)
            found = dot(strip[r], window).astype(BF16)
            for b in range(K):
                basis[r * PAD + JB * j:r * PAD + JB * j + JB, D * b:D * b + D] = found[JB * b:JB * b + JB]
    own = ext[2:4, WH:WH + PAD].reshape(CELLS, D).astype(F32)
    mixed[...] = (own + dot(basis[...], mixd[...])).astype(BF16)

    c0, c1 = 0.7978845608028654, 0.044715
    for n in range(3):
        pre[...] = dot(mixed[...], win_ref[:, 256 * n:256 * n + 256])

        def step(i, carry, n=n):
            at = pl.ds(pl.multiple_of(i * 64, 64), 64)
            p = pre[at, :]
            sq = p * p
            t = jnp.tanh(c0 * p * (1.0 + c1 * sq))
            half = 0.5 * (1.0 + t)
            hidden[at, 256 * n:256 * n + 256] = (p * half).astype(BF16)
            slope = half + 0.5 * p * (1.0 - t * t) * (c0 * (1.0 + 3.0 * c1 * sq))
            gpre[at, 256 * n:256 * n + 256] = (ghid[at, 256 * n:256 * n + 256] * slope).astype(BF16)
            return carry

        lax.fori_loop(0, CELLS // 64, step, 0)

    cots = cot[...].reshape(CELLS, D)
    gmixed[...] = (cots.astype(F32) + dot(gpre[...], win_ref[...], ((1,), (1,)))).astype(BF16)
    d_out = dot(hidden[...], cots, ((0,), (0,))).astype(BF16)
    for n in range(3):
        part[48 * n:48 * n + 48] = d_out[:, 128 * n:128 * n + 128].reshape(48, 16, 128)
    d_in = dot(mixed[...], gpre[...], ((0,), (0,))).astype(BF16)
    for n in range(6):
        part[144 + 24 * n:168 + 24 * n] = d_in[:, 128 * n:128 * n + 128].reshape(24, 16, 128)
    f_row, f_col = (lax.broadcasted_iota(jnp.int32, (D, 128), d) for d in (0, 1))
    fold = (f_col == f_row - DG * group(f_row)).astype(BF16)
    for b in range(K):
        d_mix = dot(basis[:, D * b:D * b + D], gmixed[...], ((0,), (0,)))
        d_mix = jnp.where(block, d_mix, 0.0).astype(BF16)
        part[288 + 24 * b:312 + 24 * b] = dot(d_mix, fold).astype(BF16).reshape(24, 16, 128)
    part[360:TILES] = jnp.zeros((TILES - 360, 16, 128), BF16)

    core_copy = remote(part.at[pl.ds(HALF * (1 - core), HALF)], core_in, core_s, core_r, other)
    core_copy.start()

    for b in range(K):
        gbasis[:, D * b:D * b + D] = dot(gmixed[...], mixd[D * b:D * b + D], ((1,), (1,))).astype(BF16)
    gext[...] = jnp.zeros((6, EXT, D), F32)
    for r in range(ROWS):
        for j in range(NJ):
            at = r * PAD + JB * j
            lines = jnp.concatenate([gbasis[at:at + JB, D * b:D * b + D] for b in range(K)], axis=0)
            piece = dot(strip[r], lines, ((0,), (0,)))
            gext[r:r + OFF, JB * j:JB * j + WIN] += piece.reshape(OFF, WIN, D)
    for r in range(6):
        rim_out[r] = gext[r, WH:WH + PAD].astype(BF16)
        side_out[0, r] = gext[r, 0:WH].astype(BF16)
        side_out[1, r] = pltpu.roll(gext[r, PAD:PAD + 32], 28, 0)[:WH].astype(BF16)
    rim = Halo(rim_s, rim_r)
    far_rows, near_rows = pl.ds(4 * core, 2), pl.ds(4 - 4 * core, 2)
    rims = []
    for k in range(NJ):
        rims.append(rim.copy(k, rim_out.at[far_rows, pl.ds(JB * k, JB)], rim_relay.at[:, pl.ds(JB * k, JB)], rim.relay))
    rim_near_copy = rim.copy(6, rim_out.at[near_rows], rim_near, rim.near)
    sides = [
        rim.copy(7, side_out.at[0, far_rows], side_in.at[0], rim.far_west),
        rim.copy(8, side_out.at[1, far_rows], side_in.at[1], rim.far_east),
        rim.copy(9, side_out.at[0, 2:4], side_in.at[2], rim.west),
        rim.copy(10, side_out.at[1, 2:4], side_in.at[3], rim.east),
        rim.copy(11, side_out.at[0, near_rows], side_in.at[4], rim.near_west),
        rim.copy(12, side_out.at[1, near_rows], side_in.at[5], rim.near_east),
    ]
    for c in rims + sides + [rim_near_copy]:
        c.start()

    core_copy.wait_recv()
    me = x * 4 + y
    plane = []
    for k in range(1, 16):
        q, to = plane_peer(k)
        mine = part[pl.ds(HALF * core + PER * q, PER)].astype(F32)
        half_out[pl.ds(PER * q, PER)] = (mine + core_in[pl.ds(PER * q, PER)].astype(F32)).astype(BF16)
        c = remote(half_out.at[pl.ds(PER * q, PER)], plane_in.at[k], plane_s.at[k], plane_r.at[k], to)
        c.start()
        plane.append(c)
    summed = part[pl.ds(HALF * core + PER * me, PER)].astype(F32) + core_in[pl.ds(PER * me, PER)].astype(F32)
    z_out[...] = summed

    out = mixed[...].astype(F32) + dot(hidden[...], wout_ref[...])
    for r in range(ROWS):
        out_ref[r] = out[r * PAD:r * PAD + LON].astype(BF16)
    for k in range(NJ):
        rims[k].wait_recv()
        c = rim.copy(3 + k, rim_relay.at[:, pl.ds(JB * k, JB)], rim_far.at[:, pl.ds(JB * k, JB)], rim.beyond)
        c.start()
        rims.append(c)

    for c in plane:
        c.wait_recv()
    for k in range(1, 16):
        z_out[...] += plane_in[k].astype(F32)
    for k in range(1, 16):
        pz, to = z_peer(k)

        @pl.when(pz % 4 != 3)
        def _(k=k, pz=pz, to=to):
            remote(z_out.at[(pz // 4) * 3 + pz % 4], z_in.at[k], z_s.at[k], z_r.at[k], to).start()

    tile = (z // 4) * 3 + jnp.minimum(z % 4, 2)
    owner = z % 4 != 3

    @pl.when(owner)
    def _():
        for k in range(1, 16):
            remote(z_out.at[0], z_in.at[k], z_s.at[k], z_r.at[k], other).wait_recv()
        acc = z_out[tile]
        for k in range(1, 16):
            acc += z_in[k]
        z_all[tile] = acc.astype(BF16)
        for k in range(1, 16):
            remote(z_all.at[tile], z_all.at[tile], zg_s.at[k], zg_r.at[k], z_peer(k)[1]).start()

    for k in range(1, 16):
        @pl.when((z - k + 16) % 4 != 3)
        def _(k=k):
            remote(z_all.at[0], z_all.at[0], zg_s.at[k], zg_r.at[k], other).wait_recv()

    mine_at = HALF * core + PER * me
    total[pl.ds(mine_at, PER)] = z_all[...]
    gathers = []
    for k in range(1, 16):
        gathers.append(remote(z_all, total.at[pl.ds(mine_at, PER)], pg_s.at[k], pg_r.at[k], plane_peer(k)[1]))
    mirrors = [remote(z_all, total.at[pl.ds(mine_at, PER)], cg_s.at[0], cg_r.at[0], other)]
    for c in gathers + mirrors:
        c.start()

    for k in range(NJ):
        rims[3 + k].wait_recv()
    rim_near_copy.wait_recv()
    for c in sides:
        c.wait_recv()
    gm = gmixed[...].reshape(ROWS, PAD, D).astype(F32)
    for r in range(ROWS):
        gext[2 + r, WH:WH + PAD] += gm[r] + rim_far[r].astype(F32) + rim_near[r].astype(F32)
        east = side_in[0, r].astype(F32) + side_in[2, r].astype(F32) + side_in[4, r].astype(F32)
        east = pltpu.roll(jnp.concatenate([east, jnp.zeros((WH, D), F32)], axis=0), 4, 0)
        gext[2 + r, 176:208] += east
        gext[2 + r, 16:32] += side_in[1, r].astype(F32) + side_in[3, r].astype(F32) + side_in[5, r].astype(F32)
        gfield_ref[r] = gext[2 + r, WH:WH + LON].astype(BF16)

    for k in range(1, 16):
        gathers[k - 1].wait_recv()
        qx, qy = (x + 4 - k // 4) % 4, (y + 4 - k % 4) % 4
        at = pl.ds(HALF * core + PER * (qx * 4 + qy), PER)
        c = remote(total.at[at], total.at[at], cg_s.at[k], cg_r.at[k], other)
        c.start()
        mirrors.append(c)
    for c in mirrors:
        c.wait_recv()
    for n in range(3):
        gout_ref[:, 128 * n:128 * n + 128] = total[48 * n:48 * n + 48].reshape(HID, 128)
    for n in range(6):
        gin_ref[:, 128 * n:128 * n + 128] = total[144 + 24 * n:168 + 24 * n].reshape(D, 128)
    for b in range(K):
        folded = total[288 + 24 * b:312 + 24 * b].reshape(D, 128)
        gmix_ref[b] = folded[:, :DG].reshape(G, DG, DG)

    for c in sends[NJ:] + corners + rims + sides + [rim_near_copy, core_copy] + plane + gathers + mirrors:
        c.wait_send()
    for k in range(1, 16):
        @pl.when((z + k) % 4 != 3)
        def _(k=k):
            remote(z_out.at[0], z_in.at[k], z_s.at[k], z_r.at[k], other).wait_send()

        @pl.when(owner)
        def _(k=k):
            remote(z_all.at[0], z_all.at[0], zg_s.at[k], zg_r.at[k], other).wait_send()


def body(field, row_shift, output_tile_index, tiles, mix, w_in, w_out, cotangent):
    vmem = pl.BlockSpec(memory_space=pltpu.VMEM)
    smem = pl.BlockSpec(memory_space=pltpu.SMEM)
    dma = pltpu.SemaphoreType.DMA
    v = pltpu.VMEM
    return pl.pallas_call(
        kernel,
        name="block",
        out_shape=(
            jax.ShapeDtypeStruct((ROWS, LON, D), BF16),
            jax.ShapeDtypeStruct((ROWS, LON, D), BF16),
            jax.ShapeDtypeStruct((K, G, DG, DG), BF16),
            jax.ShapeDtypeStruct((D, HID), BF16),
            jax.ShapeDtypeStruct((HID, D), BF16),
        ),
        in_specs=[smem, smem] + [vmem] * 6,
        out_specs=[vmem] * 5,
        scratch_shapes=[
            v((6, EXT, D), BF16), v((6, WH, D), BF16), v((2, WH, D), BF16), v((2, PAD, D), BF16), v((ROWS, PAD, D), BF16),
            v((32, 128), F32), v((ROWS, K * JB, OFF * WIN), BF16), v((K * D, D), BF16), v((CELLS, K * D), BF16),
            v((CELLS, D), BF16), v((CELLS, HID), BF16), v((CELLS, HID), BF16), v((CELLS, HID), F32), v((CELLS, 256), F32),
            v((CELLS, D), BF16), v((CELLS, K * D), BF16), v((6, EXT, D), F32),
            v((6, PAD, D), BF16), v((2, PAD, D), BF16), v((2, PAD, D), BF16), v((2, PAD, D), BF16),
            v((2, 6, WH, D), BF16), v((6, 2, WH, D), BF16),
            v((TILES, 16, 128), BF16), v((HALF, 16, 128), BF16), v((HALF, 16, 128), BF16), v((16, PER, 16, 128), BF16),
            v((PER, 16, 128), F32), v((16, 16, 128), F32), v((PER, 16, 128), BF16), v((TILES, 16, 128), BF16),
            dma((13,)), dma((13,)), dma((13,)), dma((13,)), dma, dma,
            dma((16,)), dma((16,)), dma((16,)), dma((16,)), dma((16,)), dma((16,)), dma((16,)), dma((16,)), dma((16,)), dma((16,)),
        ],
        compiler_params=pltpu.CompilerParams(collective_id=0, has_side_effects=True, vmem_limit_bytes=48 * 2**20),
        cost_estimate=pl.CostEstimate(flops=4 * 10**9, bytes_accessed=8 * 10**6, transcendentals=3 * 10**5),
    )(row_shift, output_tile_index, field, cotangent, tiles, mix, w_in, w_out)


def solution(mesh):
    grid = P("lat", "lon", None)
    return jax.shard_map(
        body,
        mesh=mesh,
        in_specs=(grid, P("lat"), P("lat"), P(), P(), P(), P(), grid),
        out_specs=(grid, grid, P(), P(), P()),
        check_vma=False,
    )
```

```python
import functools

import jax
import jax.numpy as jnp
from jax import lax
from jax.experimental import pallas as pl
from jax.experimental.pallas import tpu as pltpu
from jax.sharding import PartitionSpec as P

D = 384
HID = 768
G = 4
DG = 96
K = 3
WTAP = 33
NLAT = 128
WH = 16
ROWS = 2
LON = 180
PAD = 192
JB = 64
NJ = 3
MID = 48
EARLY = 2
WIN = 128
EXT = 256
OFF = 5
CELLS = ROWS * PAD
TILES = 384
PIECE = TILES // 2
HALF = PIECE // 2
PER = HALF // 16
MESH = pl.DeviceIdType.MESH
F32 = jnp.float32
BF16 = jnp.bfloat16


def dot(a, b, contract=((1,), (0,))):
    return lax.dot_general(a, b, (contract, ((), ())), preferred_element_type=F32)


def position():
    lat, lon = lax.axis_index("lat"), lax.axis_index("lon")
    return lat // 16, (lat // 4) % 4, ((lat // 2) % 2) * 8 + lon, lat % 2


def device(x, y, z, core):
    return (((x * 4 + y) * 2 + z // 8) * 2 + core, z % 8)


def remote(src, dst, send_sem, recv_sem, to):
    return pltpu.make_async_remote_copy(
        src_ref=src, dst_ref=dst, send_sem=send_sem, recv_sem=recv_sem, device_id=to, device_id_type=MESH
    )


class Halo:
    def __init__(self, sems_out, sems_in):
        lat, lon = lax.axis_index("lat"), lax.axis_index("lon")
        core = lat % 2
        step = 1 - 2 * core
        self.near = (lat + step, lon)
        self.far = ((lat + 64 - step) % 64, lon)
        west, east = (lon + 7) % 8, (lon + 1) % 8
        self.west, self.east = (lat, west), (lat, east)
        self.near_west, self.near_east = (lat + step, west), (lat + step, east)
        self.sems_out, self.sems_in = sems_out, sems_in

    def copy(self, i, src, dst, to):
        return remote(src, dst, self.sems_out.at[i], self.sems_in.at[i], to)


def kernel(
    shift_ref, index_ref, field_ref, cot_ref, tiles_ref, mix_ref, win_ref, wout_ref,
    out_ref, gfield_ref, gmix_ref, gin_ref, gout_ref,
    ext, east_in, east_out, far_east, tail_out, tail_in, cot, taps, strip, mixd, basis, mixed, hidden, gpre, ghid, pre,
    gmixed, gbasis, gext, rim_mid, far_mid, rim_ends, far_ends, rim_tail, far_tail, rim_near_out, rim_near, side_out, side_in,
    part, core_in, half_out, plane_in, z_out, z_in, z_all, total,
    halo_s, halo_r, rim_s, rim_r, core_s, core_r, plane_s, plane_r, z_s, z_r, zg_s, zg_r, pg_s, pg_r, cg_s, cg_r,
):
    x, y, z, core = position()
    lat, lon = lax.axis_index("lat"), lax.axis_index("lon")
    halo = Halo(halo_s, halo_r)
    other = device(x, y, z, 1 - core)

    def plane_peer(k):
        px, py = (x + k // 4) % 4, (y + k % 4) % 4
        return px * 4 + py, device(px, py, z, core)

    def z_peer(k):
        pz = (z + k) % 16
        return pz, device(x, y, pz, core)

    barrier = pltpu.get_barrier_semaphore()
    greet = [halo.near, halo.far, halo.west, halo.east, halo.near_west, halo.near_east]
    greet += [plane_peer(k)[1] for k in range(1, 16)] + [z_peer(k)[1] for k in range(1, 16)]
    for to in greet:
        pl.semaphore_signal(barrier, inc=1, device_id=to, device_id_type=MESH)

    ext[2:4, PAD:EXT] = jnp.zeros((2, EXT - PAD, D), BF16)
    for r in (0, 1, 4, 5):
        ext[r, WH + PAD:EXT] = jnp.zeros((EXT - WH - PAD, D), BF16)
    for r in range(ROWS):
        ext[2 + r, WH:WH + LON] = field_ref[r]
        cot[r, PAD - 16:PAD] = jnp.zeros((16, D), BF16)
        cot[r, 0:LON] = cot_ref[r]
        edge = ext[2 + r, 176:208].astype(F32)
        east_out[r] = pltpu.roll(edge, 28, 0)[:WH].astype(BF16)
    tails = [ext[2 + r, 192:208].astype(F32) for r in range(ROWS)]
    tail_out[...] = (tails[0] + pltpu.roll(tails[1], 4, 0)).astype(BF16)

    ghid[...] = dot(cot[...].reshape(CELLS, D), wout_ref[...], ((1,), (1,)))
    group = lambda n: (n >= DG).astype(jnp.int32) + (n >= 2 * DG).astype(jnp.int32) + (n >= 3 * DG).astype(jnp.int32)
    row_i, col_i = (lax.broadcasted_iota(jnp.int32, (D, D), d) for d in (0, 1))
    block = group(row_i) == group(col_i)
    s_row, s_col = (lax.broadcasted_iota(jnp.int32, (DG, D), d) for d in (0, 1))
    spread = (s_row == s_col - DG * group(s_col)).astype(BF16)
    for b in range(K):
        wide = dot(mix_ref[b].reshape(D, DG), spread)
        mixd[D * b:D * b + D] = jnp.where(block, wide, 0.0).astype(BF16)
    taps[...] = jnp.zeros((32, 128), F32)
    for r in range(ROWS):
        s, t = shift_ref[r], index_ref[r]
        for b in range(K):
            tile = tiles_ref[b, t].astype(F32)
            for o in range(OFF):
                line = jnp.zeros((1, WTAP), F32)
                here = lat * ROWS + r + o - 2
                inside = jnp.logical_and(here >= 0, here < NLAT)
                for k in range(K):
                    line = jnp.where(jnp.logical_and(inside, k == o - 1 - s), tile[k:k + 1], line)
                n = (r * K + b) * OFF + o
                taps[n:n + 1, 0:WTAP] = line
    for r in range(ROWS):
        for b in range(K):
            for o in range(OFF):
                n = (r * K + b) * OFF + o
                line = jnp.broadcast_to(taps[n:n + 1], (JB, WIN))
                strip[r, JB * b:JB * b + JB, WIN * o:WIN * o + WIN] = pltpu.roll(
                    line, 0, 1, stride=1, stride_axis=0).astype(BF16)

    pl.semaphore_wait(barrier, len(greet))

    near_at = core * 4
    far_at = 4 - core * 4
    far_here = pl.ds(core * 4, 2)
    send_w = halo.copy(3, ext.at[2:4, 16:32], ext.at[pl.ds(far_at, 2), 16:32], halo.far)
    send_e = halo.copy(4, ext.at[2:4, 176:192], ext.at[pl.ds(far_at, 2), 176:192], halo.far)
    send_t = halo.copy(5, tail_out, tail_in, halo.far)
    sends = [send_e, send_t, send_w]
    for k in range(NJ):
        at = pl.ds(2 * WH + MID * k, MID)
        sends.append(halo.copy(k, ext.at[2:4, at], ext.at[pl.ds(far_at, 2), at], halo.far))
    near = halo.copy(6, ext.at[2:4, WH:WH + PAD], ext.at[pl.ds(near_at, 2), WH:WH + PAD], halo.near)
    own_west = ext.at[2:4, 16:32]
    corners = [
        halo.copy(9, own_west, east_in.at[2:4], halo.west),
        halo.copy(10, east_out, ext.at[2:4, 0:16], halo.east),
        halo.copy(11, own_west, east_in.at[pl.ds(near_at, 2)], halo.near_west),
        halo.copy(12, east_out, ext.at[pl.ds(near_at, 2), 0:16], halo.near_east),
    ]
    for c in sends + [near] + corners:
        c.start()

    send_w.wait_recv()
    pass_w = halo.copy(7, ext.at[far_here, 16:32], east_in.at[far_here], halo.west)
    pass_w.start()
    send_e.wait_recv()
    send_t.wait_recv()
    four = lax.broadcasted_iota(jnp.int32, (WH, D), 0) < 4
    tail = tail_in[...].astype(F32)
    for r in range(ROWS):
        end = jnp.where(four, tail if r == 0 else pltpu.roll(tail, 12, 0), 0.0)
        ext[core * 4 + r, 192:208] = end.astype(BF16)
        edge = jnp.concatenate([ext[core * 4 + r, 176:192].astype(F32), end], axis=0)
        far_east[r] = pltpu.roll(edge, 28, 0)[:WH].astype(BF16)
    pass_e = halo.copy(8, far_east, ext.at[far_here, 0:16], halo.east)
    pass_e.start()

    near.wait()
    for c in sends[3:] + corners + [pass_w, pass_e]:
        c.wait_recv()
    for r in range(6):
        edge = jnp.concatenate([east_in[r].astype(F32), jnp.zeros((WH, D), F32)], axis=0)
        ext[r, PAD:PAD + 32] = (ext[r, PAD:PAD + 32].astype(F32) + pltpu.roll(edge, 4, 0)).astype(BF16)

    for r in range(ROWS):
        for j in range(NJ):
            window = ext[r:r + OFF, JB * j:JB * j + WIN].reshape(OFF * WIN, D)
            found = dot(strip[r], window).astype(BF16)
            for b in range(K):
                basis[r * PAD + JB * j:r * PAD + JB * j + JB, D * b:D * b + D] = found[JB * b:JB * b + JB]
    own = ext[2:4, WH:WH + PAD].reshape(CELLS, D).astype(F32)
    mixed[...] = (own + dot(basis[...], mixd[...])).astype(BF16)

    c0, c1 = 0.7978845608028654, 0.044715
    for n in range(3):
        pre[...] = dot(mixed[...], win_ref[:, 256 * n:256 * n + 256])

        def step(i, carry, n=n):
            at = pl.ds(pl.multiple_of(i * 64, 64), 64)
            p = pre[at, :]
            sq = p * p
            t = jnp.tanh(c0 * p * (1.0 + c1 * sq))
            half = 0.5 * (1.0 + t)
            hidden[at, 256 * n:256 * n + 256] = (p * half).astype(BF16)
            slope = half + 0.5 * p * (1.0 - t * t) * (c0 * (1.0 + 3.0 * c1 * sq))
            gpre[at, 256 * n:256 * n + 256] = (ghid[at, 256 * n:256 * n + 256] * slope).astype(BF16)
            return carry

        lax.fori_loop(0, CELLS // 64, step, 0)

    gmixed[...] = (cot[...].reshape(CELLS, D).astype(F32) + dot(gpre[...], win_ref[...], ((1,), (1,)))).astype(BF16)
    for b in range(K):
        gbasis[:, D * b:D * b + D] = dot(gmixed[...], mixd[D * b:D * b + D], ((1,), (1,))).astype(BF16)
    gext[...] = jnp.zeros((6, EXT, D), F32)
    for r in range(ROWS):
        for j in range(NJ):
            at = r * PAD + JB * j
            lines = jnp.concatenate([gbasis[at:at + JB, D * b:D * b + D] for b in range(K)], axis=0)
            piece = dot(strip[r], lines, ((0,), (0,)))
            gext[r:r + OFF, JB * j:JB * j + WIN] += piece.reshape(OFF, WIN, D)
    for r in range(6):
        side_out[0, r] = gext[r, 0:WH].astype(BF16)
        side_out[1, r] = pltpu.roll(gext[r, PAD:PAD + 32], 28, 0)[:WH].astype(BF16)
    for r in range(ROWS):
        rim_mid[r] = gext[core * 4 + r, 2 * WH:2 * WH + NJ * MID].astype(BF16)
    rim = Halo(rim_s, rim_r)
    rims = [rim.copy(9, side_out.at[0], side_in.at[0], rim.west), rim.copy(10, side_out.at[1], side_in.at[1], rim.east)]
    for k in range(NJ):
        at = pl.ds(MID * k, MID)
        rims.append(rim.copy(k, rim_mid.at[:, at], far_mid.at[:, at], rim.far))
    for c in rims[:2 + EARLY]:
        c.start()

    def core_send(p):
        c = remote(part.at[pl.ds(PIECE * p + HALF * (1 - core), HALF)], core_in.at[p], core_s.at[p], core_r.at[p], other)
        c.start()
        return c

    cots = cot[...].reshape(CELLS, D)
    d_out = dot(hidden[...], cots, ((0,), (0,))).astype(BF16)
    for n in range(3):
        part[48 * n:48 * n + 48] = d_out[:, 128 * n:128 * n + 128].reshape(48, 16, 128)

    def pack_in(n):
        d_in = dot(mixed[...], gpre[:, 256 * n:256 * n + 256], ((0,), (0,))).astype(BF16)
        for h in range(2):
            at = 144 + 24 * (2 * n + h)
            part[at:at + 24] = d_in[:, 128 * h:128 * h + 128].reshape(24, 16, 128)

    pack_in(0)
    core_copies = [core_send(0)]
    pack_in(1)
    pack_in(2)
    f_row, f_col = (lax.broadcasted_iota(jnp.int32, (D, 128), d) for d in (0, 1))
    fold = (f_col == f_row - DG * group(f_row)).astype(BF16)
    for b in range(K):
        d_mix = dot(basis[:, D * b:D * b + D], gmixed[...], ((0,), (0,)))
        d_mix = jnp.where(block, d_mix, 0.0).astype(BF16)
        part[288 + 24 * b:312 + 24 * b] = dot(d_mix, fold).astype(BF16).reshape(24, 16, 128)
    part[360:TILES] = jnp.zeros((TILES - 360, 16, 128), BF16)
    core_copies.append(core_send(1))

    me = x * 4 + y

    def core_sum(p, q):
        mine = part[pl.ds(PIECE * p + HALF * core + PER * q, PER)].astype(F32)
        return mine + core_in[p, pl.ds(PER * q, PER)].astype(F32)

    def plane_send(p):
        core_copies[p].wait_recv()
        copies = []
        for k in range(1, 16):
            q, to = plane_peer(k)
            half_out[p, pl.ds(PER * q, PER)] = core_sum(p, q).astype(BF16)
            c = remote(half_out.at[p, pl.ds(PER * q, PER)], plane_in.at[p, k], plane_s.at[p, k], plane_r.at[p, k], to)
            c.start()
            copies.append(c)
        z_out[p] = core_sum(p, me)
        return copies

    plane = [plane_send(0)]

    plane.append(plane_send(1))

    out = mixed[...].astype(F32) + dot(hidden[...], wout_ref[...])
    for r in range(ROWS):
        out_ref[r] = out[r * PAD:r * PAD + LON].astype(BF16)

    for c in rims[:2]:
        c.wait_recv()
    for r in range(6):
        gext[r, WH:2 * WH] += side_in[1, r].astype(F32)
        edge = jnp.concatenate([side_in[0, r].astype(F32), jnp.zeros((WH, D), F32)], axis=0)
        gext[r, 176:208] += pltpu.roll(edge, 4, 0)
    ends = []
    for r in range(ROWS):
        rim_near_out[r] = gext[4 - core * 4 + r, WH:WH + PAD].astype(BF16)
        rim_ends[0, r] = gext[core * 4 + r, WH:2 * WH].astype(BF16)
        rim_ends[1, r] = gext[core * 4 + r, 176:192].astype(BF16)
        ends.append(jnp.where(four, gext[core * 4 + r, 192:208], 0.0))
    rim_tail[...] = (ends[0] + pltpu.roll(ends[1], 4, 0)).astype(BF16)
    rims += [
        rim.copy(3, rim_ends, far_ends, rim.far),
        rim.copy(5, rim_tail, far_tail, rim.far),
        rim.copy(6, rim_near_out, rim_near, rim.near),
    ]
    rims[-1].start()

    def owns(p, at):
        return (at % 8 + 3 - p) % 3 == 0

    def tile_of(p, at):
        return jnp.minimum((at // 8) * 3 + jnp.maximum(at % 8 - p, 0) // 3, PER - 1)

    def z_send(p):
        for c in plane[p]:
            c.wait_recv()
        acc = z_out[p]
        for k in range(1, 16):
            acc += plane_in[p, k].astype(F32)
        z_out[p] = acc
        for k in range(1, 16):
            pz, to = z_peer(k)

            @pl.when(owns(p, pz))
            def _(k=k, pz=pz, to=to):
                remote(z_out.at[p, tile_of(p, pz)], z_in.at[p, k], z_s.at[p, k], z_r.at[p, k], to).start()

    def z_sum(p):
        tile = tile_of(p, z)

        @pl.when(owns(p, z))
        def _():
            for k in range(1, 16):
                remote(z_out.at[p, 0], z_in.at[p, k], z_s.at[p, k], z_r.at[p, k], other).wait_recv()
            acc = z_out[p, tile]
            for k in range(1, 16):
                acc += z_in[p, k]
            z_all[p, tile] = acc.astype(BF16)
            for k in range(1, 16):
                remote(z_all.at[p, tile], z_all.at[p, tile], zg_s.at[p, k], zg_r.at[p, k], z_peer(k)[1]).start()

    def mine_at(p):
        return pl.ds(PIECE * p + HALF * core + PER * me, PER)

    def gather_send(p):
        for k in range(1, 16):
            @pl.when(owns(p, (z - k + 16) % 16))
            def _(k=k):
                remote(z_all.at[p, 0], z_all.at[p, 0], zg_s.at[p, k], zg_r.at[p, k], other).wait_recv()

        total[mine_at(p)] = z_all[p]
        copies = []
        for k in range(1, 16):
            to = plane_peer(k)[1]
            copies.append(remote(z_all.at[p], total.at[mine_at(p)], pg_s.at[p, k], pg_r.at[p, k], to))
        copies.append(remote(z_all.at[p], total.at[mine_at(p)], cg_s.at[p, 0], cg_r.at[p, 0], other))
        for c in copies:
            c.start()
        return copies[:15], copies[15:]

    z_send(0)
    z_send(1)
    z_sum(0)
    z_sum(1)
    for c in rims[2 + EARLY:-1]:
        c.start()
    gathers = [gather_send(0)]
    gathers.append(gather_send(1))

    for c in rims[2:]:
        c.wait_recv()
    gm = gmixed[...].reshape(ROWS, PAD, D).astype(F32)
    tail = far_tail[...].astype(F32)
    for r in range(ROWS):
        gext[2 + r, WH:WH + PAD] += gm[r] + rim_near[r].astype(F32)
        gext[2 + r, WH:2 * WH] += far_ends[0, r].astype(F32)
        gext[2 + r, 2 * WH:176] += far_mid[r].astype(F32)
        gext[2 + r, 176:192] += far_ends[1, r].astype(F32)
        gext[2 + r, 192:208] += tail if r == 0 else pltpu.roll(tail, 12, 0)
        gfield_ref[r] = gext[2 + r, WH:WH + LON].astype(BF16)

    mirrors = gathers[0][1] + gathers[1][1]
    for p in range(2):
        for k in range(1, 16):
            gathers[p][0][k - 1].wait_recv()
            qx, qy = (x + 4 - k // 4) % 4, (y + 4 - k % 4) % 4
            at = pl.ds(PIECE * p + HALF * core + PER * (qx * 4 + qy), PER)
            c = remote(total.at[at], total.at[at], cg_s.at[p, k], cg_r.at[p, k], other)
            c.start()
            mirrors.append(c)
    for c in mirrors:
        c.wait_recv()
    for n in range(3):
        gout_ref[:, 128 * n:128 * n + 128] = total[48 * n:48 * n + 48].reshape(HID, 128)
    for n in range(6):
        gin_ref[:, 128 * n:128 * n + 128] = total[144 + 24 * n:168 + 24 * n].reshape(D, 128)
    for b in range(K):
        folded = total[288 + 24 * b:312 + 24 * b].reshape(D, 128)
        gmix_ref[b] = folded[:, :DG].reshape(G, DG, DG)

    for c in sends + corners + [pass_w, pass_e] + rims + core_copies + plane[0] + plane[1] + gathers[0][0] + gathers[1][0] + mirrors:
        c.wait_send()
    for p in range(2):
        for k in range(1, 16):
            @pl.when(owns(p, (z + k) % 16))
            def _(p=p, k=k):
                remote(z_out.at[p, 0], z_in.at[p, k], z_s.at[p, k], z_r.at[p, k], other).wait_send()

            @pl.when(owns(p, z))
            def _(p=p, k=k):
                remote(z_all.at[p, 0], z_all.at[p, 0], zg_s.at[p, k], zg_r.at[p, k], other).wait_send()


def body(field, row_shift, output_tile_index, tiles, mix, w_in, w_out, cotangent):
    vmem = pl.BlockSpec(memory_space=pltpu.VMEM)
    smem = pl.BlockSpec(memory_space=pltpu.SMEM)
    dma = pltpu.SemaphoreType.DMA
    v = pltpu.VMEM
    return pl.pallas_call(
        kernel,
        name="block",
        out_shape=(
            jax.ShapeDtypeStruct((ROWS, LON, D), BF16),
            jax.ShapeDtypeStruct((ROWS, LON, D), BF16),
            jax.ShapeDtypeStruct((K, G, DG, DG), BF16),
            jax.ShapeDtypeStruct((D, HID), BF16),
            jax.ShapeDtypeStruct((HID, D), BF16),
        ),
        in_specs=[smem, smem] + [vmem] * 6,
        out_specs=[vmem] * 5,
        scratch_shapes=[
            v((6, EXT, D), BF16), v((6, WH, D), BF16), v((2, WH, D), BF16), v((2, WH, D), BF16), v((WH, D), BF16), v((WH, D), BF16),
            v((ROWS, PAD, D), BF16),
            v((32, 128), F32), v((ROWS, K * JB, OFF * WIN), BF16), v((K * D, D), BF16), v((CELLS, K * D), BF16),
            v((CELLS, D), BF16), v((CELLS, HID), BF16), v((CELLS, HID), BF16), v((CELLS, HID), F32), v((CELLS, 256), F32),
            v((CELLS, D), BF16), v((CELLS, K * D), BF16), v((6, EXT, D), F32),
            v((2, NJ * MID, D), BF16), v((2, NJ * MID, D), BF16), v((2, 2, WH, D), BF16), v((2, 2, WH, D), BF16),
            v((WH, D), BF16), v((WH, D), BF16), v((2, PAD, D), BF16), v((2, PAD, D), BF16),
            v((2, 6, WH, D), BF16), v((2, 6, WH, D), BF16),
            v((TILES, 16, 128), BF16), v((2, HALF, 16, 128), BF16), v((2, HALF, 16, 128), BF16),
            v((2, 16, PER, 16, 128), BF16), v((2, PER, 16, 128), F32), v((2, 16, 16, 128), F32),
            v((2, PER, 16, 128), BF16), v((TILES, 16, 128), BF16),
            dma((13,)), dma((13,)), dma((13,)), dma((13,)), dma((2,)), dma((2,)),
        ] + [dma((2, 16))] * 10,
        compiler_params=pltpu.CompilerParams(collective_id=0, has_side_effects=True, vmem_limit_bytes=48 * 2**20),
        cost_estimate=pl.CostEstimate(flops=4 * 10**9, bytes_accessed=8 * 10**6, transcendentals=3 * 10**5),
    )(row_shift, output_tile_index, field, cotangent, tiles, mix, w_in, w_out)


def solution(mesh):
    grid = P("lat", "lon", None)
    return jax.shard_map(
        body,
        mesh=mesh,
        in_specs=(grid, P("lat"), P("lat"), P(), P(), P(), P(), grid),
        out_specs=(grid, grid, P(), P(), P()),
        check_vma=False,
    )
```

```python
import functools

import jax
import jax.numpy as jnp
from jax import lax
from jax.experimental import pallas as pl
from jax.experimental.pallas import tpu as pltpu
from jax.sharding import PartitionSpec as P

D = 384
HID = 768
G = 4
DG = 96
K = 3
WTAP = 33
NLAT = 128
WH = 16
ROWS = 2
LON = 180
PAD = 192
JB = 64
NJ = 3
MID = 48
EARLY = 2
WIN = 128
EXT = 256
OFF = 5
CELLS = ROWS * PAD
TILES = 384
PIECE = TILES // 2
HALF = PIECE // 2
PER = HALF // 16
MESH = pl.DeviceIdType.MESH
F32 = jnp.float32
BF16 = jnp.bfloat16


def dot(a, b, contract=((1,), (0,))):
    return lax.dot_general(a, b, (contract, ((), ())), preferred_element_type=F32)


def position():
    lat, lon = lax.axis_index("lat"), lax.axis_index("lon")
    return lat // 16, (lat // 4) % 4, ((lat // 2) % 2) * 8 + lon, lat % 2


def device(x, y, z, core):
    return (((x * 4 + y) * 2 + z // 8) * 2 + core, z % 8)


def remote(src, dst, send_sem, recv_sem, to):
    return pltpu.make_async_remote_copy(
        src_ref=src, dst_ref=dst, send_sem=send_sem, recv_sem=recv_sem, device_id=to, device_id_type=MESH
    )


class Halo:
    def __init__(self, sems_out, sems_in):
        lat, lon = lax.axis_index("lat"), lax.axis_index("lon")
        core = lat % 2
        step = 1 - 2 * core
        self.near = (lat + step, lon)
        self.far = ((lat + 64 - step) % 64, lon)
        west, east = (lon + 7) % 8, (lon + 1) % 8
        self.west, self.east = (lat, west), (lat, east)
        self.sems_out, self.sems_in = sems_out, sems_in

    def copy(self, i, src, dst, to):
        return remote(src, dst, self.sems_out.at[i], self.sems_in.at[i], to)


def kernel(
    shift_ref, index_ref, field_hbm, cot_hbm, tiles_ref, mix_hbm, win_hbm, wout_hbm,
    out_ref, gfield_ref, total,
    field_ref, cot_ref, mix_ref, win_ref, wout_ref, load_s,
    ext, east_in, east_out, far_east, tail_out, tail_in, cot, taps, strip, mixd, basis, mixed, hidden, gpre, ghid, pre,
    gmixed, gbasis, gext, rim_mid, far_mid, rim_ends, far_ends, rim_tail, far_tail, rim_near_out, rim_near, side_out, side_in,
    part, core_in, half_out, plane_in, z_out, z_in, z_all,
    halo_s, halo_r, rim_s, rim_r, core_s, core_r, plane_s, plane_r, z_s, z_r, zg_s, zg_r, pg_s, pg_r, cg_s, cg_r,
):
    x, y, z, core = position()
    lat, lon = lax.axis_index("lat"), lax.axis_index("lon")
    halo = Halo(halo_s, halo_r)
    other = device(x, y, z, 1 - core)

    def plane_peer(k):
        px, py = (x + k // 4) % 4, (y + k % 4) % 4
        return px * 4 + py, device(px, py, z, core)

    def z_peer(k):
        pz = (z + k) % 16
        return pz, device(x, y, pz, core)

    barrier = pltpu.get_barrier_semaphore()
    greet = [halo.near, halo.far, halo.west, halo.east]
    greet += [plane_peer(k)[1] for k in range(1, 16)] + [z_peer(k)[1] for k in range(1, 16)]
    for to in greet:
        pl.semaphore_signal(barrier, inc=1, device_id=to, device_id_type=MESH)

    loads = [
        pltpu.make_async_copy(src, dst, load_s.at[i])
        for i, (src, dst) in enumerate([
            (field_hbm, field_ref), (cot_hbm, cot_ref), (wout_hbm, wout_ref), (mix_hbm, mix_ref), (win_hbm, win_ref)])
    ]
    for c in loads:
        c.start()
    ext[2:4, PAD:EXT] = jnp.zeros((2, EXT - PAD, D), BF16)
    for r in (0, 1, 4, 5):
        ext[r, WH + PAD:EXT] = jnp.zeros((EXT - WH - PAD, D), BF16)
    for r in range(ROWS):
        cot[r, PAD - 16:PAD] = jnp.zeros((16, D), BF16)
    loads[0].wait()
    ext[2:4, WH:WH + LON] = jnp.swapaxes(field_ref[...], 0, 1)
    for r in range(ROWS):
        edge = ext[2 + r, 176:208].astype(F32)
        east_out[r] = pltpu.roll(edge, 28, 0)[:WH].astype(BF16)
    tails = [ext[2 + r, 192:208].astype(F32) for r in range(ROWS)]
    tail_out[...] = (tails[0] + pltpu.roll(tails[1], 4, 0)).astype(BF16)

    loads[1].wait()
    cot[:, 0:LON] = jnp.swapaxes(cot_ref[...], 0, 1)
    loads[2].wait()
    ghid[...] = dot(cot[...].reshape(CELLS, D), wout_ref[...], ((1,), (1,)))
    group = lambda n: (n >= DG).astype(jnp.int32) + (n >= 2 * DG).astype(jnp.int32) + (n >= 3 * DG).astype(jnp.int32)
    row_i, col_i = (lax.broadcasted_iota(jnp.int32, (D, D), d) for d in (0, 1))
    block = group(row_i) == group(col_i)
    s_row, s_col = (lax.broadcasted_iota(jnp.int32, (DG, D), d) for d in (0, 1))
    spread = (s_row == s_col - DG * group(s_col)).astype(BF16)
    loads[3].wait()
    for b in range(K):
        wide = dot(mix_ref[b].reshape(D, DG), spread)
        mixd[D * b:D * b + D] = jnp.where(block, wide, 0.0).astype(BF16)
    taps[...] = jnp.zeros((32, 128), F32)
    for r in range(ROWS):
        s, t = shift_ref[r], index_ref[r]
        for b in range(K):
            chosen = lax.broadcasted_iota(jnp.int32, (16, WTAP), 0) == t
            tile = [
                jnp.sum(jnp.where(chosen, tiles_ref[b, k].astype(F32), 0.0), axis=0, keepdims=True) for k in range(K)]
            for o in range(OFF):
                line = jnp.zeros((1, WTAP), F32)
                here = lat * ROWS + r + o - 2
                inside = jnp.logical_and(here >= 0, here < NLAT)
                for k in range(K):
                    line = jnp.where(jnp.logical_and(inside, k == o - 1 - s), tile[k], line)
                n = (r * K + b) * OFF + o
                taps[n:n + 1, 0:WTAP] = line
    for r in range(ROWS):
        for b in range(K):
            for o in range(OFF):
                n = (r * K + b) * OFF + o
                line = jnp.broadcast_to(taps[n:n + 1], (JB, WIN))
                strip[r, JB * b:JB * b + JB, WIN * o:WIN * o + WIN] = pltpu.roll(
                    line, 0, 1, stride=1, stride_axis=0).astype(BF16)

    gext[...] = jnp.zeros((6, EXT, D), F32)
    loads[4].wait()
    pl.semaphore_wait(barrier, len(greet))

    near_at = core * 4
    far_at = 4 - core * 4
    far_here = pl.ds(core * 4, 2)
    send_w = halo.copy(3, ext.at[2:4, 16:32], ext.at[pl.ds(far_at, 2), 16:32], halo.far)
    send_e = halo.copy(4, ext.at[2:4, 176:192], ext.at[pl.ds(far_at, 2), 176:192], halo.far)
    send_t = halo.copy(5, tail_out, tail_in, halo.far)
    sends = [send_e, send_t, send_w]
    for k in range(NJ):
        at = pl.ds(2 * WH + MID * k, MID)
        sends.append(halo.copy(k, ext.at[2:4, at], ext.at[pl.ds(far_at, 2), at], halo.far))
    near = halo.copy(6, ext.at[2:4, WH:WH + PAD], ext.at[pl.ds(near_at, 2), WH:WH + PAD], halo.near)
    own_west = ext.at[2:4, 16:32]
    corners = [
        halo.copy(9, own_west, east_in.at[2:4], halo.west),
        halo.copy(10, east_out, ext.at[2:4, 0:16], halo.east),
    ]
    for c in sends + [near] + corners:
        c.start()

    corners[0].wait_recv()
    share_w = halo.copy(11, east_in.at[2:4], east_in.at[pl.ds(near_at, 2)], halo.near)
    share_w.start()
    corners[1].wait_recv()
    share_e = halo.copy(12, ext.at[2:4, 0:16], ext.at[pl.ds(near_at, 2), 0:16], halo.near)
    share_e.start()
    send_w.wait_recv()
    pass_w = halo.copy(7, ext.at[far_here, 16:32], east_in.at[far_here], halo.west)
    pass_w.start()
    send_e.wait_recv()
    send_t.wait_recv()
    four = lax.broadcasted_iota(jnp.int32, (WH, D), 0) < 4
    tail = tail_in[...].astype(F32)
    for r in range(ROWS):
        end = jnp.where(four, tail if r == 0 else pltpu.roll(tail, 12, 0), 0.0)
        ext[core * 4 + r, 192:208] = end.astype(BF16)
        edge = jnp.concatenate([ext[core * 4 + r, 176:192].astype(F32), end], axis=0)
        far_east[r] = pltpu.roll(edge, 28, 0)[:WH].astype(BF16)
    pass_e = halo.copy(8, far_east, ext.at[far_here, 0:16], halo.east)
    pass_e.start()

    near.wait()
    for c in sends[3:] + [share_w, share_e, pass_w, pass_e]:
        c.wait_recv()
    for r in range(6):
        edge = jnp.concatenate([east_in[r].astype(F32), jnp.zeros((WH, D), F32)], axis=0)
        ext[r, PAD:PAD + 32] = (ext[r, PAD:PAD + 32].astype(F32) + pltpu.roll(edge, 4, 0)).astype(BF16)

    for r in range(ROWS):
        for j in range(NJ):
            window = ext[r:r + OFF, JB * j:JB * j + WIN].reshape(OFF * WIN, D)
            found = dot(strip[r], window).astype(BF16)
            for b in range(K):
                basis[r * PAD + JB * j:r * PAD + JB * j + JB, D * b:D * b + D] = found[JB * b:JB * b + JB]
    own = ext[2:4, WH:WH + PAD].reshape(CELLS, D).astype(F32)
    mixed[...] = (own + dot(basis[...], mixd[...])).astype(BF16)

    c0, c1 = 0.7978845608028654, 0.044715
    for n in range(3):
        pre[...] = dot(mixed[...], win_ref[:, 256 * n:256 * n + 256])

        def step(i, carry, n=n):
            at = pl.ds(pl.multiple_of(i * 64, 64), 64)
            p = pre[at, :]
            sq = p * p
            t = jnp.tanh(c0 * p * (1.0 + c1 * sq))
            half = 0.5 * (1.0 + t)
            hidden[at, 256 * n:256 * n + 256] = (p * half).astype(BF16)
            slope = half + 0.5 * p * (1.0 - t * t) * (c0 * (1.0 + 3.0 * c1 * sq))
            gpre[at, 256 * n:256 * n + 256] = (ghid[at, 256 * n:256 * n + 256] * slope).astype(BF16)
            return carry

        lax.fori_loop(0, CELLS // 64, step, 0)

    gmixed[...] = (cot[...].reshape(CELLS, D).astype(F32) + dot(gpre[...], win_ref[...], ((1,), (1,)))).astype(BF16)
    for b in range(K):
        gbasis[:, D * b:D * b + D] = dot(gmixed[...], mixd[D * b:D * b + D], ((1,), (1,))).astype(BF16)

    def adjoint(r, first, last):
        for j in range(NJ):
            at = r * PAD + JB * j
            lines = jnp.concatenate([gbasis[at:at + JB, D * b:D * b + D] for b in range(K)], axis=0)
            piece = dot(strip[r, :, WIN * first:WIN * last], lines, ((0,), (0,)))
            gext[r + first:r + last, JB * j:JB * j + WIN] += piece.reshape(last - first, WIN, D)

    @pl.when(core == 0)
    def _():
        adjoint(0, 0, 2)
        adjoint(1, 0, 1)

    @pl.when(core == 1)
    def _():
        adjoint(0, 4, 5)
        adjoint(1, 3, 5)

    for r in range(ROWS):
        rim_mid[r] = gext[core * 4 + r, 2 * WH:2 * WH + NJ * MID].astype(BF16)
    rim = Halo(rim_s, rim_r)
    rims = [rim.copy(9, side_out.at[0], side_in.at[0], rim.west), rim.copy(10, side_out.at[1], side_in.at[1], rim.east)]
    for k in range(NJ):
        at = pl.ds(MID * k, MID)
        rims.append(rim.copy(k, rim_mid.at[:, at], far_mid.at[:, at], rim.far))
    for c in rims[2:2 + EARLY]:
        c.start()

    @pl.when(core == 0)
    def _():
        adjoint(0, 2, 5)
        adjoint(1, 1, 5)

    @pl.when(core == 1)
    def _():
        adjoint(0, 0, 4)
        adjoint(1, 0, 3)

    for r in range(6):
        side_out[0, r] = gext[r, 0:WH].astype(BF16)
        side_out[1, r] = pltpu.roll(gext[r, PAD:PAD + 32], 28, 0)[:WH].astype(BF16)
    for c in rims[:2]:
        c.start()

    def core_send(p):
        c = remote(part.at[pl.ds(PIECE * p + HALF * (1 - core), HALF)], core_in.at[p], core_s.at[p], core_r.at[p], other)
        c.start()
        return c

    cots = cot[...].reshape(CELLS, D)
    d_out = dot(hidden[...], cots, ((0,), (0,))).astype(BF16)
    for n in range(3):
        part[48 * n:48 * n + 48] = d_out[:, 128 * n:128 * n + 128].reshape(48, 16, 128)

    def pack_in(n):
        d_in = dot(mixed[...], gpre[:, 256 * n:256 * n + 256], ((0,), (0,))).astype(BF16)
        for h in range(2):
            at = 144 + 24 * (2 * n + h)
            part[at:at + 24] = d_in[:, 128 * h:128 * h + 128].reshape(24, 16, 128)

    pack_in(0)
    core_copies = [core_send(0)]
    pack_in(1)
    pack_in(2)
    f_row, f_col = (lax.broadcasted_iota(jnp.int32, (D, 128), d) for d in (0, 1))
    fold = (f_col == f_row - DG * group(f_row)).astype(BF16)
    for b in range(K):
        d_mix = dot(basis[:, D * b:D * b + D], gmixed[...], ((0,), (0,)))
        d_mix = jnp.where(block, d_mix, 0.0).astype(BF16)
        part[288 + 24 * b:312 + 24 * b] = dot(d_mix, fold).astype(BF16).reshape(24, 16, 128)
    part[360:TILES] = jnp.zeros((TILES - 360, 16, 128), BF16)
    core_copies.append(core_send(1))

    me = x * 4 + y

    def core_sum(p, q):
        mine = part[pl.ds(PIECE * p + HALF * core + PER * q, PER)].astype(F32)
        return mine + core_in[p, pl.ds(PER * q, PER)].astype(F32)

    def plane_send(p):
        core_copies[p].wait_recv()
        copies = []
        for k in range(1, 16):
            q, to = plane_peer(k)
            half_out[p, pl.ds(PER * q, PER)] = core_sum(p, q).astype(BF16)
            c = remote(half_out.at[p, pl.ds(PER * q, PER)], plane_in.at[p, k], plane_s.at[p, k], plane_r.at[p, k], to)
            c.start()
            copies.append(c)
        z_out[p] = core_sum(p, me)
        return copies

    plane = [plane_send(0)]

    plane.append(plane_send(1))

    out = mixed[...].astype(F32) + dot(hidden[...], wout_ref[...])
    for r in range(ROWS):
        out_ref[r] = out[r * PAD:r * PAD + LON].astype(BF16)

    for c in rims[:2]:
        c.wait_recv()
    for r in range(6):
        gext[r, WH:2 * WH] += side_in[1, r].astype(F32)
        edge = jnp.concatenate([side_in[0, r].astype(F32), jnp.zeros((WH, D), F32)], axis=0)
        gext[r, 176:208] += pltpu.roll(edge, 4, 0)
    ends = []
    for r in range(ROWS):
        rim_near_out[r] = gext[4 - core * 4 + r, WH:WH + PAD].astype(BF16)
        rim_ends[0, r] = gext[core * 4 + r, WH:2 * WH].astype(BF16)
        rim_ends[1, r] = gext[core * 4 + r, 176:192].astype(BF16)
        ends.append(jnp.where(four, gext[core * 4 + r, 192:208], 0.0))
    rim_tail[...] = (ends[0] + pltpu.roll(ends[1], 4, 0)).astype(BF16)
    rims += [
        rim.copy(3, rim_ends, far_ends, rim.far),
        rim.copy(5, rim_tail, far_tail, rim.far),
        rim.copy(6, rim_near_out, rim_near, rim.near),
    ]
    rims[-1].start()

    def owns(p, at):
        return (at % 8 + 3 - p) % 3 == 0

    def tile_of(p, at):
        return jnp.minimum((at // 8) * 3 + jnp.maximum(at % 8 - p, 0) // 3, PER - 1)

    def z_send(p):
        for c in plane[p]:
            c.wait_recv()
        acc = z_out[p]
        for k in range(1, 16):
            acc += plane_in[p, k].astype(F32)
        z_out[p] = acc
        for k in range(1, 16):
            pz, to = z_peer(k)

            @pl.when(owns(p, pz))
            def _(k=k, pz=pz, to=to):
                remote(z_out.at[p, tile_of(p, pz)], z_in.at[p, k], z_s.at[p, k], z_r.at[p, k], to).start()

    def z_sum(p):
        tile = tile_of(p, z)

        @pl.when(owns(p, z))
        def _():
            for k in range(1, 16):
                remote(z_out.at[p, 0], z_in.at[p, k], z_s.at[p, k], z_r.at[p, k], other).wait_recv()
            acc = z_out[p, tile]
            for k in range(1, 16):
                acc += z_in[p, k]
            z_all[p, tile] = acc.astype(BF16)
            for k in range(1, 16):
                remote(z_all.at[p, tile], z_all.at[p, tile], zg_s.at[p, k], zg_r.at[p, k], z_peer(k)[1]).start()

    def mine_at(p):
        return pl.ds(PIECE * p + HALF * core + PER * me, PER)

    def gather_send(p):
        for k in range(1, 16):
            @pl.when(owns(p, (z - k + 16) % 16))
            def _(k=k):
                remote(z_all.at[p, 0], z_all.at[p, 0], zg_s.at[p, k], zg_r.at[p, k], other).wait_recv()

        total[mine_at(p)] = z_all[p]
        copies = []
        for k in range(1, 16):
            to = plane_peer(k)[1]
            copies.append(remote(z_all.at[p], total.at[mine_at(p)], pg_s.at[p, k], pg_r.at[p, k], to))
        copies.append(remote(z_all.at[p], total.at[mine_at(p)], cg_s.at[p, 0], cg_r.at[p, 0], other))
        for c in copies:
            c.start()
        return copies[:15], copies[15:]

    z_send(0)
    z_send(1)
    z_sum(0)
    z_sum(1)
    gathers = [gather_send(0)]
    gathers.append(gather_send(1))
    for c in rims[2 + EARLY:-1]:
        c.start()

    for c in rims[2:]:
        c.wait_recv()
    gm = gmixed[...].reshape(ROWS, PAD, D).astype(F32)
    tail = far_tail[...].astype(F32)
    for r in range(ROWS):
        gext[2 + r, WH:WH + PAD] += gm[r] + rim_near[r].astype(F32)
        gext[2 + r, WH:2 * WH] += far_ends[0, r].astype(F32)
        gext[2 + r, 2 * WH:176] += far_mid[r].astype(F32)
        gext[2 + r, 176:192] += far_ends[1, r].astype(F32)
        gext[2 + r, 192:208] += tail if r == 0 else pltpu.roll(tail, 12, 0)
        gfield_ref[r] = gext[2 + r, WH:WH + LON].astype(BF16)

    mirrors = gathers[0][1] + gathers[1][1]
    for p in range(2):
        for k in range(1, 16):
            gathers[p][0][k - 1].wait_recv()
            qx, qy = (x + 4 - k // 4) % 4, (y + 4 - k % 4) % 4
            at = pl.ds(PIECE * p + HALF * core + PER * (qx * 4 + qy), PER)
            c = remote(total.at[at], total.at[at], cg_s.at[p, k], cg_r.at[p, k], other)
            c.start()
            mirrors.append(c)
    for c in mirrors:
        c.wait_recv()
    for c in sends + corners + [share_w, share_e, pass_w, pass_e] + rims + core_copies + plane[0] + plane[1] + gathers[0][0] + gathers[1][0] + mirrors:
        c.wait_send()
    for p in range(2):
        for k in range(1, 16):
            @pl.when(owns(p, (z + k) % 16))
            def _(p=p, k=k):
                remote(z_out.at[p, 0], z_in.at[p, k], z_s.at[p, k], z_r.at[p, k], other).wait_send()

            @pl.when(owns(p, z))
            def _(p=p, k=k):
                remote(z_all.at[p, 0], z_all.at[p, 0], zg_s.at[p, k], zg_r.at[p, k], other).wait_send()


def unpack(total, out_in, gfield_in, out_ref, gfield_ref, gmix_ref, gin_ref, gout_ref):
    for n in range(3):
        gout_ref[:, 128 * n:128 * n + 128] = total[48 * n:48 * n + 48].reshape(HID, 128)
    for n in range(6):
        gin_ref[:, 128 * n:128 * n + 128] = total[144 + 24 * n:168 + 24 * n].reshape(D, 128)
    for b in range(K):
        folded = total[288 + 24 * b:312 + 24 * b].reshape(D, 128)
        gmix_ref[b] = folded[:, :DG].reshape(G, DG, DG)
    out_ref[...] = jnp.swapaxes(out_in[...], 0, 1)
    gfield_ref[...] = jnp.swapaxes(gfield_in[...], 0, 1)


def body(field, row_shift, output_tile_index, tiles, mix, w_in, w_out, cotangent):
    vmem = pl.BlockSpec(memory_space=pltpu.VMEM)
    smem = pl.BlockSpec(memory_space=pltpu.SMEM)
    anywhere = pl.BlockSpec(memory_space=pltpu.HBM)
    dma = pltpu.SemaphoreType.DMA
    v = pltpu.VMEM
    out, gfield, total = pl.pallas_call(
        kernel,
        name="block",
        out_shape=(
            jax.ShapeDtypeStruct((ROWS, LON, D), BF16),
            jax.ShapeDtypeStruct((ROWS, LON, D), BF16),
            jax.ShapeDtypeStruct((TILES, 16, 128), BF16),
        ),
        in_specs=[smem, smem, anywhere, anywhere, vmem, anywhere, anywhere, anywhere],
        out_specs=[vmem] * 3,
        scratch_shapes=[
            v((LON, ROWS, D), BF16), v((LON, ROWS, D), BF16), v((K, G, DG, DG), BF16), v((D, HID), BF16), v((HID, D), BF16),
            dma((5,)),
            v((6, EXT, D), BF16), v((6, WH, D), BF16), v((2, WH, D), BF16), v((2, WH, D), BF16), v((WH, D), BF16), v((WH, D), BF16),
            v((ROWS, PAD, D), BF16),
            v((32, 128), F32), v((ROWS, K * JB, OFF * WIN), BF16), v((K * D, D), BF16), v((CELLS, K * D), BF16),
            v((CELLS, D), BF16), v((CELLS, HID), BF16), v((CELLS, HID), BF16), v((CELLS, HID), F32), v((CELLS, 256), F32),
            v((CELLS, D), BF16), v((CELLS, K * D), BF16), v((6, EXT, D), F32),
            v((2, NJ * MID, D), BF16), v((2, NJ * MID, D), BF16), v((2, 2, WH, D), BF16), v((2, 2, WH, D), BF16),
            v((WH, D), BF16), v((WH, D), BF16), v((2, PAD, D), BF16), v((2, PAD, D), BF16),
            v((2, 6, WH, D), BF16), v((2, 6, WH, D), BF16),
            v((TILES, 16, 128), BF16), v((2, HALF, 16, 128), BF16), v((2, HALF, 16, 128), BF16),
            v((2, 16, PER, 16, 128), BF16), v((2, PER, 16, 128), F32), v((2, 16, 16, 128), F32), v((2, PER, 16, 128), BF16),
            dma((13,)), dma((13,)), dma((13,)), dma((13,)), dma((2,)), dma((2,)),
        ] + [dma((2, 16))] * 10,
        compiler_params=pltpu.CompilerParams(collective_id=0, has_side_effects=True, vmem_limit_bytes=60 * 2**20),
        cost_estimate=pl.CostEstimate(flops=4 * 10**9, bytes_accessed=8 * 10**6, transcendentals=3 * 10**5),
    )(row_shift, output_tile_index, jnp.swapaxes(field, 0, 1), jnp.swapaxes(cotangent, 0, 1), jnp.swapaxes(tiles, 1, 2), mix, w_in, w_out)
    out, gfield, gmix, gin, gout = pl.pallas_call(
        unpack,
        name="unpack",
        out_shape=(
            jax.ShapeDtypeStruct((LON, ROWS, D), BF16),
            jax.ShapeDtypeStruct((LON, ROWS, D), BF16),
            jax.ShapeDtypeStruct((K, G, DG, DG), BF16),
            jax.ShapeDtypeStruct((D, HID), BF16),
            jax.ShapeDtypeStruct((HID, D), BF16),
        ),
        in_specs=[vmem] * 3,
        out_specs=[vmem] * 5,
        compiler_params=pltpu.CompilerParams(vmem_limit_bytes=60 * 2**20),
    )(total, out, gfield)
    return jnp.swapaxes(out, 0, 1), jnp.swapaxes(gfield, 0, 1), gmix, gin, gout


def solution(mesh):
    grid = P("lat", "lon", None)
    return jax.shard_map(
        body,
        mesh=mesh,
        in_specs=(grid, P("lat"), P("lat"), P(), P(), P(), P(), grid),
        out_specs=(grid, grid, P(), P(), P()),
        check_vma=False,
    )
```

```python
import functools

import jax
import jax.numpy as jnp
from jax import lax
from jax.experimental import pallas as pl
from jax.experimental.pallas import tpu as pltpu
from jax.sharding import PartitionSpec as P

D = 384
HID = 768
G = 4
DG = 96
K = 3
WTAP = 33
NLAT = 128
WH = 16
ROWS = 2
LON = 180
PAD = 192
JB = 64
NJ = 3
MID = 48
EARLY = 2
WIN = 128
EXT = 256
OFF = 5
CELLS = ROWS * PAD
TILES = 384
PIECE = TILES // 2
HALF = PIECE // 2
PER = HALF // 16
MESH = pl.DeviceIdType.MESH
F32 = jnp.float32
BF16 = jnp.bfloat16


def dot(a, b, contract=((1,), (0,))):
    return lax.dot_general(a, b, (contract, ((), ())), preferred_element_type=F32)


def position():
    lat, lon = lax.axis_index("lat"), lax.axis_index("lon")
    return lat // 16, (lat // 4) % 4, ((lat // 2) % 2) * 8 + lon, lat % 2


def device(x, y, z, core):
    return (((x * 4 + y) * 2 + z // 8) * 2 + core, z % 8)


def remote(src, dst, send_sem, recv_sem, to):
    return pltpu.make_async_remote_copy(
        src_ref=src, dst_ref=dst, send_sem=send_sem, recv_sem=recv_sem, device_id=to, device_id_type=MESH
    )


class Halo:
    def __init__(self, sems_out, sems_in):
        lat, lon = lax.axis_index("lat"), lax.axis_index("lon")
        core = lat % 2
        step = 1 - 2 * core
        self.near = (lat + step, lon)
        self.far = ((lat + 64 - step) % 64, lon)
        west, east = (lon + 7) % 8, (lon + 1) % 8
        self.west, self.east = (lat, west), (lat, east)
        self.near_west, self.near_east = (lat + step, west), (lat + step, east)
        self.sems_out, self.sems_in = sems_out, sems_in

    def copy(self, i, src, dst, to):
        return remote(src, dst, self.sems_out.at[i], self.sems_in.at[i], to)


def kernel(
    shift_ref, index_ref, field_hbm, cot_hbm, tiles_ref, mix_hbm, win_hbm, wout_hbm,
    out_ref, gfield_ref, total,
    field_ref, cot_ref, mix_ref, win_ref, wout_ref, load_s,
    ext, east_in, east_out, far_east, tail_out, tail_in, begun, cot, taps, strip, mixd, basis, mixed, hidden, gpre, ghid, pre,
    gmixed, gbasis, gext, rim_mid, far_mid, rim_ends, far_ends, rim_tail, far_tail, rim_near_out, rim_near, side_out, side_in,
    part, core_in, half_out, plane_in, z_out, z_half, z_in, z_all,
    halo_s, halo_r, rim_s, rim_r, core_s, core_r, plane_s, plane_r, z_s, z_r, zg_s, zg_r, pg_s, pg_r, cg_s, cg_r,
):
    x, y, z, core = position()
    lat, lon = lax.axis_index("lat"), lax.axis_index("lon")
    halo = Halo(halo_s, halo_r)
    other = device(x, y, z, 1 - core)

    def plane_peer(k):
        px, py = (x + k // 4) % 4, (y + k % 4) % 4
        return px * 4 + py, device(px, py, z, core)

    def z_peer(k):
        pz = (z + k) % 16
        return pz, device(x, y, pz, core)

    barrier = pltpu.get_barrier_semaphore()
    greet = [halo.near, halo.far, halo.west, halo.east, halo.near_west, halo.near_east]
    greet += [plane_peer(k)[1] for k in range(1, 16)] + [z_peer(k)[1] for k in range(1, 16)]
    for to in greet:
        pl.semaphore_signal(barrier, inc=1, device_id=to, device_id_type=MESH)

    loads = [
        pltpu.make_async_copy(src, dst, load_s.at[i])
        for i, (src, dst) in enumerate([
            (field_hbm, field_ref), (cot_hbm, cot_ref), (wout_hbm, wout_ref), (mix_hbm, mix_ref), (win_hbm, win_ref)])
    ]
    for c in loads:
        c.start()
    ext[2:4, PAD:EXT] = jnp.zeros((2, EXT - PAD, D), BF16)
    for r in (0, 1, 4, 5):
        ext[r, WH + PAD:EXT] = jnp.zeros((EXT - WH - PAD, D), BF16)
    for r in range(ROWS):
        cot[r, PAD - 16:PAD] = jnp.zeros((16, D), BF16)
    loads[0].wait()
    ext[2:4, WH:WH + LON] = jnp.swapaxes(field_ref[...], 0, 1)
    for r in range(ROWS):
        edge = ext[2 + r, 176:208].astype(F32)
        east_out[r] = pltpu.roll(edge, 28, 0)[:WH].astype(BF16)
    tails = [ext[2 + r, 192:208].astype(F32) for r in range(ROWS)]
    tail_out[...] = (tails[0] + pltpu.roll(tails[1], 4, 0)).astype(BF16)

    pl.semaphore_wait(barrier, len(greet))

    near_at = core * 4
    far_at = 4 - core * 4
    far_here = pl.ds(core * 4, 2)
    send_w = halo.copy(3, ext.at[2:4, 16:32], ext.at[pl.ds(far_at, 2), 16:32], halo.far)
    send_e = halo.copy(4, ext.at[2:4, 176:192], ext.at[pl.ds(far_at, 2), 176:192], halo.far)
    send_t = halo.copy(5, tail_out, tail_in, halo.far)
    sends = [send_e, send_t, send_w]
    for k in range(NJ):
        at = pl.ds(2 * WH + MID * k, MID)
        sends.append(halo.copy(k, ext.at[2:4, at], ext.at[pl.ds(far_at, 2), at], halo.far))
    near = halo.copy(6, ext.at[2:4, WH:WH + PAD], ext.at[pl.ds(near_at, 2), WH:WH + PAD], halo.near)
    own_west = ext.at[2:4, 16:32]
    corners = [
        halo.copy(9, own_west, east_in.at[2:4], halo.west),
        halo.copy(10, east_out, ext.at[2:4, 0:16], halo.east),
        halo.copy(11, own_west, east_in.at[pl.ds(near_at, 2)], halo.near_west),
        halo.copy(12, east_out, ext.at[pl.ds(near_at, 2), 0:16], halo.near_east),
    ]
    for c in sends + [near] + corners:
        c.start()

    loads[1].wait()
    cot[:, 0:LON] = jnp.swapaxes(cot_ref[...], 0, 1)
    loads[2].wait()
    ghid[...] = dot(cot[...].reshape(CELLS, D), wout_ref[...], ((1,), (1,)))
    group = lambda n: (n >= DG).astype(jnp.int32) + (n >= 2 * DG).astype(jnp.int32) + (n >= 3 * DG).astype(jnp.int32)
    row_i, col_i = (lax.broadcasted_iota(jnp.int32, (D, D), d) for d in (0, 1))
    block = group(row_i) == group(col_i)
    s_row, s_col = (lax.broadcasted_iota(jnp.int32, (DG, D), d) for d in (0, 1))
    spread = (s_row == s_col - DG * group(s_col)).astype(BF16)
    loads[3].wait()
    for b in range(K):
        wide = dot(mix_ref[b].reshape(D, DG), spread)
        mixd[D * b:D * b + D] = jnp.where(block, wide, 0.0).astype(BF16)
    taps[...] = jnp.zeros((32, 128), F32)
    for r in range(ROWS):
        s, t = shift_ref[r], index_ref[r]
        for b in range(K):
            chosen = lax.broadcasted_iota(jnp.int32, (16, WTAP), 0) == t
            tile = [
                jnp.sum(jnp.where(chosen, tiles_ref[b, k].astype(F32), 0.0), axis=0, keepdims=True) for k in range(K)]
            for o in range(OFF):
                line = jnp.zeros((1, WTAP), F32)
                here = lat * ROWS + r + o - 2
                inside = jnp.logical_and(here >= 0, here < NLAT)
                for k in range(K):
                    line = jnp.where(jnp.logical_and(inside, k == o - 1 - s), tile[k], line)
                n = (r * K + b) * OFF + o
                taps[n:n + 1, 0:WTAP] = line
    for r in range(ROWS):
        for b in range(K):
            for o in range(OFF):
                n = (r * K + b) * OFF + o
                line = jnp.broadcast_to(taps[n:n + 1], (JB, WIN))
                strip[r, JB * b:JB * b + JB, WIN * o:WIN * o + WIN] = pltpu.roll(
                    line, 0, 1, stride=1, stride_axis=0).astype(BF16)

    gext[...] = jnp.zeros((6, EXT, D), F32)
    loads[4].wait()

    send_w.wait_recv()
    pass_w = halo.copy(7, ext.at[far_here, 16:32], east_in.at[far_here], halo.west)
    pass_w.start()
    send_e.wait_recv()
    send_t.wait_recv()
    four = lax.broadcasted_iota(jnp.int32, (WH, D), 0) < 4
    tail = tail_in[...].astype(F32)
    for r in range(ROWS):
        end = jnp.where(four, tail if r == 0 else pltpu.roll(tail, 12, 0), 0.0)
        ext[core * 4 + r, 192:208] = end.astype(BF16)
        edge = jnp.concatenate([ext[core * 4 + r, 176:192].astype(F32), end], axis=0)
        far_east[r] = pltpu.roll(edge, 28, 0)[:WH].astype(BF16)
    pass_e = halo.copy(8, far_east, ext.at[far_here, 0:16], halo.east)
    pass_e.start()

    def east_edge(r):
        edge = jnp.concatenate([east_in[r].astype(F32), jnp.zeros((WH, D), F32)], axis=0)
        ext[r, PAD:PAD + 32] = (ext[r, PAD:PAD + 32].astype(F32) + pltpu.roll(edge, 4, 0)).astype(BF16)

    def filtered(r, j, first, last):
        window = ext[r + first:r + last, JB * j:JB * j + WIN].reshape((last - first) * WIN, D)
        return dot(strip[r, :, WIN * first:WIN * last], window)

    near.wait()
    for c in corners:
        c.wait_recv()
    for r in (2, 3):
        east_edge(r)
    for r in range(2):
        east_edge(4 - core * 4 + r)
    for c, ranges in ((0, ((2, 5), (1, 5))), (1, ((0, 4), (0, 3)))):
        @pl.when(core == c)
        def _(ranges=ranges):
            for r in range(ROWS):
                for j in range(NJ):
                    begun[r * NJ + j] = filtered(r, j, *ranges[r])

    for c in sends[3:] + [pass_w, pass_e]:
        c.wait_recv()
    for r in range(2):
        east_edge(core * 4 + r)

    for c, ranges in ((0, ((0, 2), (0, 1))), (1, ((4, 5), (3, 5)))):
        @pl.when(core == c)
        def _(ranges=ranges):
            for r in range(ROWS):
                for j in range(NJ):
                    found = (begun[r * NJ + j] + filtered(r, j, *ranges[r])).astype(BF16)
                    for b in range(K):
                        basis[r * PAD + JB * j:r * PAD + JB * j + JB, D * b:D * b + D] = found[JB * b:JB * b + JB]
    own = ext[2:4, WH:WH + PAD].reshape(CELLS, D).astype(F32)
    mixed[...] = (own + dot(basis[...], mixd[...])).astype(BF16)

    c0, c1 = 0.7978845608028654, 0.044715
    for n in range(3):
        pre[...] = dot(mixed[...], win_ref[:, 256 * n:256 * n + 256])

        def step(i, carry, n=n):
            at = pl.ds(pl.multiple_of(i * 64, 64), 64)
            p = pre[at, :]
            sq = p * p
            t = jnp.tanh(c0 * p * (1.0 + c1 * sq))
            half = 0.5 * (1.0 + t)
            hidden[at, 256 * n:256 * n + 256] = (p * half).astype(BF16)
            slope = half + 0.5 * p * (1.0 - t * t) * (c0 * (1.0 + 3.0 * c1 * sq))
            gpre[at, 256 * n:256 * n + 256] = (ghid[at, 256 * n:256 * n + 256] * slope).astype(BF16)
            return carry

        lax.fori_loop(0, CELLS // 64, step, 0)

    gmixed[...] = (cot[...].reshape(CELLS, D).astype(F32) + dot(gpre[...], win_ref[...], ((1,), (1,)))).astype(BF16)
    for b in range(K):
        gbasis[:, D * b:D * b + D] = dot(gmixed[...], mixd[D * b:D * b + D], ((1,), (1,))).astype(BF16)

    def adjoint(r, first, last):
        for j in range(NJ):
            at = r * PAD + JB * j
            lines = jnp.concatenate([gbasis[at:at + JB, D * b:D * b + D] for b in range(K)], axis=0)
            piece = dot(strip[r, :, WIN * first:WIN * last], lines, ((0,), (0,)))
            gext[r + first:r + last, JB * j:JB * j + WIN] += piece.reshape(last - first, WIN, D)

    @pl.when(core == 0)
    def _():
        adjoint(0, 0, 2)
        adjoint(1, 0, 1)

    @pl.when(core == 1)
    def _():
        adjoint(0, 4, 5)
        adjoint(1, 3, 5)

    for r in range(ROWS):
        rim_mid[r] = gext[core * 4 + r, 2 * WH:2 * WH + NJ * MID].astype(BF16)
    rim = Halo(rim_s, rim_r)
    rims = [rim.copy(9, side_out.at[0], side_in.at[0], rim.west), rim.copy(10, side_out.at[1], side_in.at[1], rim.east)]
    for k in range(NJ):
        at = pl.ds(MID * k, MID)
        rims.append(rim.copy(k, rim_mid.at[:, at], far_mid.at[:, at], rim.far))
    for c in rims[2:2 + EARLY]:
        c.start()

    @pl.when(core == 0)
    def _():
        adjoint(0, 2, 5)
        adjoint(1, 1, 5)

    @pl.when(core == 1)
    def _():
        adjoint(0, 0, 4)
        adjoint(1, 0, 3)

    for r in range(6):
        side_out[0, r] = gext[r, 0:WH].astype(BF16)
        side_out[1, r] = pltpu.roll(gext[r, PAD:PAD + 32], 28, 0)[:WH].astype(BF16)
    for c in rims[:2]:
        c.start()

    def core_send(p):
        c = remote(part.at[pl.ds(PIECE * p + HALF * (1 - core), HALF)], core_in.at[p], core_s.at[p], core_r.at[p], other)
        c.start()
        return c

    cots = cot[...].reshape(CELLS, D)
    d_out = dot(hidden[...], cots, ((0,), (0,))).astype(BF16)
    for n in range(3):
        part[48 * n:48 * n + 48] = d_out[:, 128 * n:128 * n + 128].reshape(48, 16, 128)

    def pack_in(n):
        d_in = dot(mixed[...], gpre[:, 256 * n:256 * n + 256], ((0,), (0,))).astype(BF16)
        for h in range(2):
            at = 144 + 24 * (2 * n + h)
            part[at:at + 24] = d_in[:, 128 * h:128 * h + 128].reshape(24, 16, 128)

    pack_in(0)
    core_copies = [core_send(0)]
    pack_in(1)
    pack_in(2)
    f_row, f_col = (lax.broadcasted_iota(jnp.int32, (D, 128), d) for d in (0, 1))
    fold = (f_col == f_row - DG * group(f_row)).astype(BF16)
    for b in range(K):
        d_mix = dot(basis[:, D * b:D * b + D], gmixed[...], ((0,), (0,)))
        d_mix = jnp.where(block, d_mix, 0.0).astype(BF16)
        part[288 + 24 * b:312 + 24 * b] = dot(d_mix, fold).astype(BF16).reshape(24, 16, 128)
    part[360:TILES] = jnp.zeros((TILES - 360, 16, 128), BF16)
    core_copies.append(core_send(1))

    me = x * 4 + y

    def core_sum(p, q):
        mine = part[pl.ds(PIECE * p + HALF * core + PER * q, PER)].astype(F32)
        return mine + core_in[p, pl.ds(PER * q, PER)].astype(F32)

    def plane_send(p):
        core_copies[p].wait_recv()
        copies = []
        for k in range(1, 16):
            q, to = plane_peer(k)
            half_out[p, pl.ds(PER * q, PER)] = core_sum(p, q).astype(BF16)
            c = remote(half_out.at[p, pl.ds(PER * q, PER)], plane_in.at[p, k], plane_s.at[p, k], plane_r.at[p, k], to)
            c.start()
            copies.append(c)
        z_out[p] = core_sum(p, me)
        return copies

    plane = [plane_send(0)]

    plane.append(plane_send(1))

    out = mixed[...].astype(F32) + dot(hidden[...], wout_ref[...])
    for r in range(ROWS):
        out_ref[r] = out[r * PAD:r * PAD + LON].astype(BF16)

    for c in rims[:2]:
        c.wait_recv()
    for r in range(6):
        gext[r, WH:2 * WH] += side_in[1, r].astype(F32)
        edge = jnp.concatenate([side_in[0, r].astype(F32), jnp.zeros((WH, D), F32)], axis=0)
        gext[r, 176:208] += pltpu.roll(edge, 4, 0)
    ends = []
    for r in range(ROWS):
        rim_near_out[r] = gext[4 - core * 4 + r, WH:WH + PAD].astype(BF16)
        rim_ends[0, r] = gext[core * 4 + r, WH:2 * WH].astype(BF16)
        rim_ends[1, r] = gext[core * 4 + r, 176:192].astype(BF16)
        ends.append(jnp.where(four, gext[core * 4 + r, 192:208], 0.0))
    rim_tail[...] = (ends[0] + pltpu.roll(ends[1], 4, 0)).astype(BF16)
    rims += [
        rim.copy(3, rim_ends, far_ends, rim.far),
        rim.copy(5, rim_tail, far_tail, rim.far),
        rim.copy(6, rim_near_out, rim_near, rim.near),
    ]
    rims[-1].start()

    def owns(p, at):
        return (at % 8 + 3 - p) % 3 == 0

    def tile_of(p, at):
        return jnp.minimum((at // 8) * 3 + jnp.maximum(at % 8 - p, 0) // 3, PER - 1)

    def z_send(p):
        for c in plane[p]:
            c.wait_recv()
        acc = z_out[p]
        for k in range(1, 16):
            acc += plane_in[p, k].astype(F32)
        z_out[p] = acc
        z_half[p] = acc.astype(BF16)
        for k in range(1, 16):
            pz, to = z_peer(k)

            @pl.when(owns(p, pz))
            def _(k=k, pz=pz, to=to):
                remote(z_half.at[p, tile_of(p, pz)], z_in.at[p, k], z_s.at[p, k], z_r.at[p, k], to).start()

    def z_sum(p):
        tile = tile_of(p, z)

        @pl.when(owns(p, z))
        def _():
            for k in range(1, 16):
                remote(z_half.at[p, 0], z_in.at[p, k], z_s.at[p, k], z_r.at[p, k], other).wait_recv()
            acc = z_out[p, tile]
            for k in range(1, 16):
                acc += z_in[p, k].astype(F32)
            z_all[p, tile] = acc.astype(BF16)
            for k in range(1, 16):
                remote(z_all.at[p, tile], z_all.at[p, tile], zg_s.at[p, k], zg_r.at[p, k], z_peer(k)[1]).start()

    def mine_at(p):
        return pl.ds(PIECE * p + HALF * core + PER * me, PER)

    def gather_send(p):
        for k in range(1, 16):
            @pl.when(owns(p, (z - k + 16) % 16))
            def _(k=k):
                remote(z_all.at[p, 0], z_all.at[p, 0], zg_s.at[p, k], zg_r.at[p, k], other).wait_recv()

        total[mine_at(p)] = z_all[p]
        copies = []
        for k in range(1, 16):
            to = plane_peer(k)[1]
            copies.append(remote(z_all.at[p], total.at[mine_at(p)], pg_s.at[p, k], pg_r.at[p, k], to))
        copies.append(remote(z_all.at[p], total.at[mine_at(p)], cg_s.at[p, 0], cg_r.at[p, 0], other))
        for c in copies:
            c.start()
        return copies[:15], copies[15:]

    z_send(0)
    z_send(1)
    z_sum(0)
    z_sum(1)
    for c in rims[2 + EARLY:-1]:
        c.start()
    gathers = [gather_send(0)]
    gathers.append(gather_send(1))

    for c in rims[2:]:
        c.wait_recv()
    gm = gmixed[...].reshape(ROWS, PAD, D).astype(F32)
    tail = far_tail[...].astype(F32)
    for r in range(ROWS):
        gext[2 + r, WH:WH + PAD] += gm[r] + rim_near[r].astype(F32)
        gext[2 + r, WH:2 * WH] += far_ends[0, r].astype(F32)
        gext[2 + r, 2 * WH:176] += far_mid[r].astype(F32)
        gext[2 + r, 176:192] += far_ends[1, r].astype(F32)
        gext[2 + r, 192:208] += tail if r == 0 else pltpu.roll(tail, 12, 0)
        gfield_ref[r] = gext[2 + r, WH:WH + LON].astype(BF16)

    mirrors = gathers[0][1] + gathers[1][1]
    for p in range(2):
        for k in range(1, 16):
            gathers[p][0][k - 1].wait_recv()
            qx, qy = (x + 4 - k // 4) % 4, (y + 4 - k % 4) % 4
            at = pl.ds(PIECE * p + HALF * core + PER * (qx * 4 + qy), PER)
            c = remote(total.at[at], total.at[at], cg_s.at[p, k], cg_r.at[p, k], other)
            c.start()
            mirrors.append(c)
    for c in mirrors:
        c.wait_recv()
    for c in sends + corners + [pass_w, pass_e] + rims + core_copies + plane[0] + plane[1] + gathers[0][0] + gathers[1][0] + mirrors:
        c.wait_send()
    for p in range(2):
        for k in range(1, 16):
            @pl.when(owns(p, (z + k) % 16))
            def _(p=p, k=k):
                remote(z_half.at[p, 0], z_in.at[p, k], z_s.at[p, k], z_r.at[p, k], other).wait_send()

            @pl.when(owns(p, z))
            def _(p=p, k=k):
                remote(z_all.at[p, 0], z_all.at[p, 0], zg_s.at[p, k], zg_r.at[p, k], other).wait_send()


def unpack(total, out_in, gfield_in, out_ref, gfield_ref, gmix_ref, gin_ref, gout_ref):
    for n in range(3):
        gout_ref[:, 128 * n:128 * n + 128] = total[48 * n:48 * n + 48].reshape(HID, 128)
    for n in range(6):
        gin_ref[:, 128 * n:128 * n + 128] = total[144 + 24 * n:168 + 24 * n].reshape(D, 128)
    for b in range(K):
        folded = total[288 + 24 * b:312 + 24 * b].reshape(D, 128)
        gmix_ref[b] = folded[:, :DG].reshape(G, DG, DG)
    out_ref[...] = jnp.swapaxes(out_in[...], 0, 1)
    gfield_ref[...] = jnp.swapaxes(gfield_in[...], 0, 1)


def body(field, row_shift, output_tile_index, tiles, mix, w_in, w_out, cotangent):
    vmem = pl.BlockSpec(memory_space=pltpu.VMEM)
    smem = pl.BlockSpec(memory_space=pltpu.SMEM)
    anywhere = pl.BlockSpec(memory_space=pltpu.HBM)
    dma = pltpu.SemaphoreType.DMA
    v = pltpu.VMEM
    field, cotangent, tiles = (jnp.swapaxes(a, *axes) for a, axes in ((field, (0, 1)), (cotangent, (0, 1)), (tiles, (1, 2))))
    row_shift, output_tile_index, field, cotangent, tiles, mix, w_in, w_out = (
        pltpu.with_memory_space_constraint(a, pltpu.HBM)
        for a in (row_shift, output_tile_index, field, cotangent, tiles, mix, w_in, w_out))
    out, gfield, total = pl.pallas_call(
        kernel,
        name="block",
        out_shape=(
            jax.ShapeDtypeStruct((ROWS, LON, D), BF16),
            jax.ShapeDtypeStruct((ROWS, LON, D), BF16),
            jax.ShapeDtypeStruct((TILES, 16, 128), BF16),
        ),
        in_specs=[smem, smem, anywhere, anywhere, vmem, anywhere, anywhere, anywhere],
        out_specs=[vmem] * 3,
        scratch_shapes=[
            v((LON, ROWS, D), BF16), v((LON, ROWS, D), BF16), v((K, G, DG, DG), BF16), v((D, HID), BF16), v((HID, D), BF16),
            dma((5,)),
            v((6, EXT, D), BF16), v((6, WH, D), BF16), v((2, WH, D), BF16), v((2, WH, D), BF16), v((WH, D), BF16), v((WH, D), BF16),
            v((ROWS * NJ, K * JB, D), F32), v((ROWS, PAD, D), BF16),
            v((32, 128), F32), v((ROWS, K * JB, OFF * WIN), BF16), v((K * D, D), BF16), v((CELLS, K * D), BF16),
            v((CELLS, D), BF16), v((CELLS, HID), BF16), v((CELLS, HID), BF16), v((CELLS, HID), F32), v((CELLS, 256), F32),
            v((CELLS, D), BF16), v((CELLS, K * D), BF16), v((6, EXT, D), F32),
            v((2, NJ * MID, D), BF16), v((2, NJ * MID, D), BF16), v((2, 2, WH, D), BF16), v((2, 2, WH, D), BF16),
            v((WH, D), BF16), v((WH, D), BF16), v((2, PAD, D), BF16), v((2, PAD, D), BF16),
            v((2, 6, WH, D), BF16), v((2, 6, WH, D), BF16),
            v((TILES, 16, 128), BF16), v((2, HALF, 16, 128), BF16), v((2, HALF, 16, 128), BF16),
            v((2, 16, PER, 16, 128), BF16), v((2, PER, 16, 128), F32), v((2, PER, 16, 128), BF16),
            v((2, 16, 16, 128), BF16), v((2, PER, 16, 128), BF16),
            dma((13,)), dma((13,)), dma((13,)), dma((13,)), dma((2,)), dma((2,)),
        ] + [dma((2, 16))] * 10,
        compiler_params=pltpu.CompilerParams(collective_id=0, has_side_effects=True, vmem_limit_bytes=48 * 2**20),
        cost_estimate=pl.CostEstimate(flops=4 * 10**9, bytes_accessed=8 * 10**6, transcendentals=3 * 10**5),
    )(row_shift, output_tile_index, field, cotangent, tiles, mix, w_in, w_out)
    out, gfield, gmix, gin, gout = pl.pallas_call(
        unpack,
        name="unpack",
        out_shape=(
            jax.ShapeDtypeStruct((LON, ROWS, D), BF16),
            jax.ShapeDtypeStruct((LON, ROWS, D), BF16),
            jax.ShapeDtypeStruct((K, G, DG, DG), BF16),
            jax.ShapeDtypeStruct((D, HID), BF16),
            jax.ShapeDtypeStruct((HID, D), BF16),
        ),
        in_specs=[vmem] * 3,
        out_specs=[vmem] * 5,
        compiler_params=pltpu.CompilerParams(vmem_limit_bytes=48 * 2**20),
    )(total, out, gfield)
    return jnp.swapaxes(out, 0, 1), jnp.swapaxes(gfield, 0, 1), gmix, gin, gout


def solution(mesh):
    grid = P("lat", "lon", None)
    return jax.shard_map(
        body,
        mesh=mesh,
        in_specs=(grid, P("lat"), P("lat"), P(), P(), P(), P(), grid),
        out_specs=(grid, grid, P(), P(), P()),
        check_vma=False,
    )
```

```python
import functools

import jax
import jax.numpy as jnp
from jax import lax
from jax.experimental import pallas as pl
from jax.experimental.pallas import tpu as pltpu
from jax.sharding import PartitionSpec as P

D = 384
HID = 768
G = 4
DG = 96
K = 3
WTAP = 33
NLAT = 128
WH = 16
ROWS = 2
LON = 180
PAD = 192
JB = 64
NJ = 3
MID = 48
EARLY = 2
WIN = 128
EXT = 256
OFF = 5
CELLS = ROWS * PAD
TILES = 384
PIECE = TILES // 2
HALF = PIECE // 2
PER = HALF // 16
MESH = pl.DeviceIdType.MESH
F32 = jnp.float32
BF16 = jnp.bfloat16


def dot(a, b, contract=((1,), (0,))):
    return lax.dot_general(a, b, (contract, ((), ())), preferred_element_type=F32)


def position():
    lat, lon = lax.axis_index("lat"), lax.axis_index("lon")
    return lat // 16, (lat // 4) % 4, ((lat // 2) % 2) * 8 + lon, lat % 2


def device(x, y, z, core):
    return (((x * 4 + y) * 2 + z // 8) * 2 + core, z % 8)


def remote(src, dst, send_sem, recv_sem, to):
    return pltpu.make_async_remote_copy(
        src_ref=src, dst_ref=dst, send_sem=send_sem, recv_sem=recv_sem, device_id=to, device_id_type=MESH
    )


class Halo:
    def __init__(self, sems_out, sems_in):
        lat, lon = lax.axis_index("lat"), lax.axis_index("lon")
        core = lat % 2
        step = 1 - 2 * core
        self.near = (lat + step, lon)
        self.far = ((lat + 64 - step) % 64, lon)
        west, east = (lon + 7) % 8, (lon + 1) % 8
        self.west, self.east = (lat, west), (lat, east)
        self.near_west, self.near_east = (lat + step, west), (lat + step, east)
        self.sems_out, self.sems_in = sems_out, sems_in

    def copy(self, i, src, dst, to):
        return remote(src, dst, self.sems_out.at[i], self.sems_in.at[i], to)


def kernel(
    shift_ref, index_ref, field_hbm, cot_hbm, tiles_ref, mix_hbm, win_hbm, wout_hbm,
    out_ref, gfield_ref, total,
    field_ref, cot_ref, mix_ref, win_ref, wout_ref, load_s,
    ext, east_in, east_out, far_east, tail_out, tail_in, begun, cot, taps, strip, mixd, basis, mixed, hidden, gpre, ghid, pre,
    gmixed, gbasis, gext, rim_mid, far_mid, rim_ends, far_ends, rim_tail, far_tail, rim_near_out, rim_near, side_out, side_in,
    part, core_in, half_out, plane_in, z_out, z_half, z_in, z_all,
    halo_s, halo_r, rim_s, rim_r, core_s, core_r, plane_s, plane_r, z_s, z_r, zg_s, zg_r, pg_s, pg_r, cg_s, cg_r,
):
    x, y, z, core = position()
    lat, lon = lax.axis_index("lat"), lax.axis_index("lon")
    halo = Halo(halo_s, halo_r)
    other = device(x, y, z, 1 - core)

    def plane_peer(k):
        px, py = (x + k // 4) % 4, (y + k % 4) % 4
        return px * 4 + py, device(px, py, z, core)

    def z_peer(k):
        pz = (z + k) % 16
        return pz, device(x, y, pz, core)

    barrier = pltpu.get_barrier_semaphore()
    greet = [halo.near, halo.far, halo.west, halo.east, halo.near_west, halo.near_east]
    greet += [plane_peer(k)[1] for k in range(1, 16)] + [z_peer(k)[1] for k in range(1, 16)]
    for to in greet:
        pl.semaphore_signal(barrier, inc=1, device_id=to, device_id_type=MESH)

    loads = [
        pltpu.make_async_copy(src, dst, load_s.at[i])
        for i, (src, dst) in enumerate([
            (field_hbm, field_ref), (cot_hbm, cot_ref), (wout_hbm, wout_ref), (mix_hbm, mix_ref), (win_hbm, win_ref)])
    ]
    for c in loads:
        c.start()
    ext[2:4, PAD:EXT] = jnp.zeros((2, EXT - PAD, D), BF16)
    for r in (0, 1, 4, 5):
        ext[r, WH + PAD:EXT] = jnp.zeros((EXT - WH - PAD, D), BF16)
    for r in range(ROWS):
        cot[r, PAD - 16:PAD] = jnp.zeros((16, D), BF16)
    loads[0].wait()
    ext[2:4, WH:WH + LON] = jnp.swapaxes(field_ref[...], 0, 1)
    for r in range(ROWS):
        edge = ext[2 + r, 176:208].astype(F32)
        east_out[r] = pltpu.roll(edge, 28, 0)[:WH].astype(BF16)
    tails = [ext[2 + r, 192:208].astype(F32) for r in range(ROWS)]
    tail_out[...] = (tails[0] + pltpu.roll(tails[1], 4, 0)).astype(BF16)

    pl.semaphore_wait(barrier, len(greet))

    near_at = core * 4
    far_at = 4 - core * 4
    far_here = pl.ds(core * 4, 2)
    send_w = halo.copy(3, ext.at[2:4, 16:32], ext.at[pl.ds(far_at, 2), 16:32], halo.far)
    send_e = halo.copy(4, ext.at[2:4, 176:192], ext.at[pl.ds(far_at, 2), 176:192], halo.far)
    send_t = halo.copy(5, tail_out, tail_in, halo.far)
    sends = [send_e, send_t, send_w]
    for k in range(NJ):
        at = pl.ds(2 * WH + MID * k, MID)
        sends.append(halo.copy(k, ext.at[2:4, at], ext.at[pl.ds(far_at, 2), at], halo.far))
    near = halo.copy(6, ext.at[2:4, WH:WH + PAD], ext.at[pl.ds(near_at, 2), WH:WH + PAD], halo.near)
    own_west = ext.at[2:4, 16:32]
    corners = [
        halo.copy(9, own_west, east_in.at[2:4], halo.west),
        halo.copy(10, east_out, ext.at[2:4, 0:16], halo.east),
        halo.copy(11, own_west, east_in.at[pl.ds(near_at, 2)], halo.near_west),
        halo.copy(12, east_out, ext.at[pl.ds(near_at, 2), 0:16], halo.near_east),
    ]
    for c in sends + [near] + corners:
        c.start()

    loads[1].wait()
    cot[:, 0:LON] = jnp.swapaxes(cot_ref[...], 0, 1)
    loads[2].wait()
    ghid[...] = dot(cot[...].reshape(CELLS, D), wout_ref[...], ((1,), (1,)))
    group = lambda n: (n >= DG).astype(jnp.int32) + (n >= 2 * DG).astype(jnp.int32) + (n >= 3 * DG).astype(jnp.int32)
    row_i, col_i = (lax.broadcasted_iota(jnp.int32, (D, D), d) for d in (0, 1))
    block = group(row_i) == group(col_i)
    s_row, s_col = (lax.broadcasted_iota(jnp.int32, (DG, D), d) for d in (0, 1))
    spread = (s_row == s_col - DG * group(s_col)).astype(BF16)
    loads[3].wait()
    for b in range(K):
        wide = dot(mix_ref[b].reshape(D, DG), spread)
        mixd[D * b:D * b + D] = jnp.where(block, wide, 0.0).astype(BF16)
    taps[...] = jnp.zeros((32, 128), F32)
    for r in range(ROWS):
        s, t = shift_ref[r], index_ref[r]
        for b in range(K):
            chosen = lax.broadcasted_iota(jnp.int32, (16, WTAP), 0) == t
            tile = [
                jnp.sum(jnp.where(chosen, tiles_ref[b, k].astype(F32), 0.0), axis=0, keepdims=True) for k in range(K)]
            for o in range(OFF):
                line = jnp.zeros((1, WTAP), F32)
                here = lat * ROWS + r + o - 2
                inside = jnp.logical_and(here >= 0, here < NLAT)
                for k in range(K):
                    line = jnp.where(jnp.logical_and(inside, k == o - 1 - s), tile[k], line)
                n = (r * K + b) * OFF + o
                taps[n:n + 1, 0:WTAP] = line
    for r in range(ROWS):
        for b in range(K):
            for o in range(OFF):
                n = (r * K + b) * OFF + o
                line = jnp.broadcast_to(taps[n:n + 1], (JB, WIN))
                strip[r, JB * b:JB * b + JB, WIN * o:WIN * o + WIN] = pltpu.roll(
                    line, 0, 1, stride=1, stride_axis=0).astype(BF16)

    gext[...] = jnp.zeros((6, EXT, D), F32)
    loads[4].wait()

    send_w.wait_recv()
    pass_w = halo.copy(7, ext.at[far_here, 16:32], east_in.at[far_here], halo.west)
    pass_w.start()
    send_e.wait_recv()
    send_t.wait_recv()
    four = lax.broadcasted_iota(jnp.int32, (WH, D), 0) < 4
    tail = tail_in[...].astype(F32)
    for r in range(ROWS):
        end = jnp.where(four, tail if r == 0 else pltpu.roll(tail, 12, 0), 0.0)
        ext[core * 4 + r, 192:208] = end.astype(BF16)
        edge = jnp.concatenate([ext[core * 4 + r, 176:192].astype(F32), end], axis=0)
        far_east[r] = pltpu.roll(edge, 28, 0)[:WH].astype(BF16)
    pass_e = halo.copy(8, far_east, ext.at[far_here, 0:16], halo.east)
    pass_e.start()

    def east_edge(r):
        edge = jnp.concatenate([east_in[r].astype(F32), jnp.zeros((WH, D), F32)], axis=0)
        ext[r, PAD:PAD + 32] = (ext[r, PAD:PAD + 32].astype(F32) + pltpu.roll(edge, 4, 0)).astype(BF16)

    def filtered(r, j, first, last):
        window = ext[r + first:r + last, JB * j:JB * j + WIN].reshape((last - first) * WIN, D)
        return dot(strip[r, :, WIN * first:WIN * last], window)

    near.wait()
    for c in corners:
        c.wait_recv()
    for r in (2, 3):
        east_edge(r)
    for r in range(2):
        east_edge(4 - core * 4 + r)
    for c, ranges in ((0, ((2, 5), (1, 5))), (1, ((0, 4), (0, 3)))):
        @pl.when(core == c)
        def _(ranges=ranges):
            for r in range(ROWS):
                for j in range(NJ):
                    begun[r * NJ + j] = filtered(r, j, *ranges[r])

    for c in sends[3:] + [pass_w, pass_e]:
        c.wait_recv()
    for r in range(2):
        east_edge(core * 4 + r)

    for c, ranges in ((0, ((0, 2), (0, 1))), (1, ((4, 5), (3, 5)))):
        @pl.when(core == c)
        def _(ranges=ranges):
            for r in range(ROWS):
                for j in range(NJ):
                    found = (begun[r * NJ + j] + filtered(r, j, *ranges[r])).astype(BF16)
                    for b in range(K):
                        basis[r * PAD + JB * j:r * PAD + JB * j + JB, D * b:D * b + D] = found[JB * b:JB * b + JB]
    own = ext[2:4, WH:WH + PAD].reshape(CELLS, D).astype(F32)
    mixed[...] = (own + dot(basis[...], mixd[...])).astype(BF16)

    c0, c1 = 0.7978845608028654, 0.044715
    for n in range(3):
        pre[...] = dot(mixed[...], win_ref[:, 256 * n:256 * n + 256])

        def step(i, carry, n=n):
            at = pl.ds(pl.multiple_of(i * 64, 64), 64)
            p = pre[at, :]
            sq = p * p
            t = jnp.tanh(c0 * p * (1.0 + c1 * sq))
            half = 0.5 * (1.0 + t)
            hidden[at, 256 * n:256 * n + 256] = (p * half).astype(BF16)
            slope = half + 0.5 * p * (1.0 - t * t) * (c0 * (1.0 + 3.0 * c1 * sq))
            gpre[at, 256 * n:256 * n + 256] = (ghid[at, 256 * n:256 * n + 256] * slope).astype(BF16)
            return carry

        lax.fori_loop(0, CELLS // 64, step, 0)

    gmixed[...] = (cot[...].reshape(CELLS, D).astype(F32) + dot(gpre[...], win_ref[...], ((1,), (1,)))).astype(BF16)
    for b in range(K):
        gbasis[:, D * b:D * b + D] = dot(gmixed[...], mixd[D * b:D * b + D], ((1,), (1,))).astype(BF16)

    def adjoint(r, first, last):
        for j in range(NJ):
            at = r * PAD + JB * j
            lines = jnp.concatenate([gbasis[at:at + JB, D * b:D * b + D] for b in range(K)], axis=0)
            piece = dot(strip[r, :, WIN * first:WIN * last], lines, ((0,), (0,)))
            gext[r + first:r + last, JB * j:JB * j + WIN] += piece.reshape(last - first, WIN, D)

    @pl.when(core == 0)
    def _():
        adjoint(0, 0, 2)
        adjoint(1, 0, 1)

    @pl.when(core == 1)
    def _():
        adjoint(0, 4, 5)
        adjoint(1, 3, 5)

    for r in range(ROWS):
        rim_mid[r] = gext[core * 4 + r, 2 * WH:2 * WH + NJ * MID].astype(BF16)
    rim = Halo(rim_s, rim_r)
    rims = [rim.copy(9, side_out.at[0], side_in.at[0], rim.west), rim.copy(10, side_out.at[1], side_in.at[1], rim.east)]
    for k in range(NJ):
        at = pl.ds(MID * k, MID)
        rims.append(rim.copy(k, rim_mid.at[:, at], far_mid.at[:, at], rim.far))
    for c in rims[2:2 + EARLY]:
        c.start()

    @pl.when(core == 0)
    def _():
        adjoint(0, 2, 5)
        adjoint(1, 1, 5)

    @pl.when(core == 1)
    def _():
        adjoint(0, 0, 4)
        adjoint(1, 0, 3)

    for r in range(6):
        side_out[0, r] = gext[r, 0:WH].astype(BF16)
        side_out[1, r] = pltpu.roll(gext[r, PAD:PAD + 32], 28, 0)[:WH].astype(BF16)
    for c in rims[:2]:
        c.start()

    def core_send(p):
        c = remote(part.at[pl.ds(PIECE * p + HALF * (1 - core), HALF)], core_in.at[p], core_s.at[p], core_r.at[p], other)
        c.start()
        return c

    cots = cot[...].reshape(CELLS, D)
    d_out = dot(hidden[...], cots, ((0,), (0,))).astype(BF16)
    for n in range(3):
        part[48 * n:48 * n + 48] = d_out[:, 128 * n:128 * n + 128].reshape(48, 16, 128)

    def pack_in(n):
        d_in = dot(mixed[...], gpre[:, 256 * n:256 * n + 256], ((0,), (0,))).astype(BF16)
        for h in range(2):
            at = 144 + 24 * (2 * n + h)
            part[at:at + 24] = d_in[:, 128 * h:128 * h + 128].reshape(24, 16, 128)

    pack_in(0)
    core_copies = [core_send(0)]
    pack_in(1)
    pack_in(2)
    f_row, f_col = (lax.broadcasted_iota(jnp.int32, (D, 128), d) for d in (0, 1))
    fold = (f_col == f_row - DG * group(f_row)).astype(BF16)
    for b in range(K):
        d_mix = dot(basis[:, D * b:D * b + D], gmixed[...], ((0,), (0,)))
        d_mix = jnp.where(block, d_mix, 0.0).astype(BF16)
        part[288 + 24 * b:312 + 24 * b] = dot(d_mix, fold).astype(BF16).reshape(24, 16, 128)
    part[360:TILES] = jnp.zeros((TILES - 360, 16, 128), BF16)
    core_copies.append(core_send(1))

    me = x * 4 + y

    def core_sum(p, q):
        mine = part[pl.ds(PIECE * p + HALF * core + PER * q, PER)].astype(F32)
        return mine + core_in[p, pl.ds(PER * q, PER)].astype(F32)

    def plane_send(p):
        core_copies[p].wait_recv()
        copies = []
        for k in range(1, 16):
            q, to = plane_peer(k)
            half_out[p, pl.ds(PER * q, PER)] = core_sum(p, q).astype(BF16)
            c = remote(half_out.at[p, pl.ds(PER * q, PER)], plane_in.at[p, k], plane_s.at[p, k], plane_r.at[p, k], to)
            c.start()
            copies.append(c)
        z_out[p] = core_sum(p, me)
        return copies

    plane = [plane_send(0)]

    plane.append(plane_send(1))

    out = mixed[...].astype(F32) + dot(hidden[...], wout_ref[...])
    for r in range(ROWS):
        out_ref[r] = out[r * PAD:r * PAD + LON].astype(BF16)

    for c in rims[:2]:
        c.wait_recv()
    for r in range(6):
        gext[r, WH:2 * WH] += side_in[1, r].astype(F32)
        edge = jnp.concatenate([side_in[0, r].astype(F32), jnp.zeros((WH, D), F32)], axis=0)
        gext[r, 176:208] += pltpu.roll(edge, 4, 0)
    ends = []
    for r in range(ROWS):
        rim_near_out[r] = gext[4 - core * 4 + r, WH:WH + PAD].astype(BF16)
        rim_ends[0, r] = gext[core * 4 + r, WH:2 * WH].astype(BF16)
        rim_ends[1, r] = gext[core * 4 + r, 176:192].astype(BF16)
        ends.append(jnp.where(four, gext[core * 4 + r, 192:208], 0.0))
    rim_tail[...] = (ends[0] + pltpu.roll(ends[1], 4, 0)).astype(BF16)
    rims += [
        rim.copy(3, rim_ends, far_ends, rim.far),
        rim.copy(5, rim_tail, far_tail, rim.far),
        rim.copy(6, rim_near_out, rim_near, rim.near),
    ]
    rims[-1].start()

    def owns(p, at):
        return (at % 8 + 3 - p) % 3 == 0

    def tile_of(p, at):
        return jnp.minimum((at // 8) * 3 + jnp.maximum(at % 8 - p, 0) // 3, PER - 1)

    def z_send(p):
        for c in plane[p]:
            c.wait_recv()
        acc = z_out[p]
        for k in range(1, 16):
            acc += plane_in[p, k].astype(F32)
        z_out[p] = acc
        z_half[p] = acc.astype(BF16)
        for k in range(1, 16):
            pz, to = z_peer(k)

            @pl.when(owns(p, pz))
            def _(k=k, pz=pz, to=to):
                remote(z_half.at[p, tile_of(p, pz)], z_in.at[p, k], z_s.at[p, k], z_r.at[p, k], to).start()

    def z_sum(p):
        tile = tile_of(p, z)

        @pl.when(owns(p, z))
        def _():
            for k in range(1, 16):
                remote(z_half.at[p, 0], z_in.at[p, k], z_s.at[p, k], z_r.at[p, k], other).wait_recv()
            acc = z_out[p, tile]
            for k in range(1, 16):
                acc += z_in[p, k].astype(F32)
            z_all[p, tile] = acc.astype(BF16)
            for k in range(1, 16):
                remote(z_all.at[p, tile], z_all.at[p, tile], zg_s.at[p, k], zg_r.at[p, k], z_peer(k)[1]).start()

    def mine_at(p):
        return pl.ds(PIECE * p + HALF * core + PER * me, PER)

    def gather_send(p):
        for k in range(1, 16):
            @pl.when(owns(p, (z - k + 16) % 16))
            def _(k=k):
                remote(z_all.at[p, 0], z_all.at[p, 0], zg_s.at[p, k], zg_r.at[p, k], other).wait_recv()

        total[mine_at(p)] = z_all[p]
        copies = []
        for k in range(1, 16):
            to = plane_peer(k)[1]
            copies.append(remote(z_all.at[p], total.at[mine_at(p)], pg_s.at[p, k], pg_r.at[p, k], to))
        copies.append(remote(z_all.at[p], total.at[mine_at(p)], cg_s.at[p, 0], cg_r.at[p, 0], other))
        for c in copies:
            c.start()
        return copies[:15], copies[15:]

    z_send(0)
    z_send(1)
    z_sum(0)
    z_sum(1)
    for c in rims[2 + EARLY:-1]:
        c.start()
    gathers = [gather_send(0)]
    gathers.append(gather_send(1))

    mirrors = gathers[0][1] + gathers[1][1]
    for p in range(2):
        for k in range(1, 16):
            gathers[p][0][k - 1].wait_recv()
            qx, qy = (x + 4 - k // 4) % 4, (y + 4 - k % 4) % 4
            at = pl.ds(PIECE * p + HALF * core + PER * (qx * 4 + qy), PER)
            c = remote(total.at[at], total.at[at], cg_s.at[p, k], cg_r.at[p, k], other)
            c.start()
            mirrors.append(c)
    for c in rims[2:]:
        c.wait_recv()
    gm = gmixed[...].reshape(ROWS, PAD, D).astype(F32)
    tail = far_tail[...].astype(F32)
    for r in range(ROWS):
        gext[2 + r, WH:WH + PAD] += gm[r] + rim_near[r].astype(F32)
        gext[2 + r, WH:2 * WH] += far_ends[0, r].astype(F32)
        gext[2 + r, 2 * WH:176] += far_mid[r].astype(F32)
        gext[2 + r, 176:192] += far_ends[1, r].astype(F32)
        gext[2 + r, 192:208] += tail if r == 0 else pltpu.roll(tail, 12, 0)
        gfield_ref[r] = gext[2 + r, WH:WH + LON].astype(BF16)

    for c in mirrors:
        c.wait_recv()
    for c in sends + corners + [pass_w, pass_e] + rims + core_copies + plane[0] + plane[1] + gathers[0][0] + gathers[1][0] + mirrors:
        c.wait_send()
    for p in range(2):
        for k in range(1, 16):
            @pl.when(owns(p, (z + k) % 16))
            def _(p=p, k=k):
                remote(z_half.at[p, 0], z_in.at[p, k], z_s.at[p, k], z_r.at[p, k], other).wait_send()

            @pl.when(owns(p, z))
            def _(p=p, k=k):
                remote(z_all.at[p, 0], z_all.at[p, 0], zg_s.at[p, k], zg_r.at[p, k], other).wait_send()


def unpack(total, out_in, gfield_in, out_ref, gfield_ref, gmix_ref, gin_ref, gout_ref):
    for n in range(3):
        gout_ref[:, 128 * n:128 * n + 128] = total[48 * n:48 * n + 48].reshape(HID, 128)
    for n in range(6):
        gin_ref[:, 128 * n:128 * n + 128] = total[144 + 24 * n:168 + 24 * n].reshape(D, 128)
    for b in range(K):
        folded = total[288 + 24 * b:312 + 24 * b].reshape(D, 128)
        gmix_ref[b] = folded[:, :DG].reshape(G, DG, DG)
    out_ref[...] = jnp.swapaxes(out_in[...], 0, 1)
    gfield_ref[...] = jnp.swapaxes(gfield_in[...], 0, 1)


def body(field, row_shift, output_tile_index, tiles, mix, w_in, w_out, cotangent):
    vmem = pl.BlockSpec(memory_space=pltpu.VMEM)
    smem = pl.BlockSpec(memory_space=pltpu.SMEM)
    anywhere = pl.BlockSpec(memory_space=pltpu.HBM)
    dma = pltpu.SemaphoreType.DMA
    v = pltpu.VMEM
    field, cotangent, tiles = (jnp.swapaxes(a, *axes) for a, axes in ((field, (0, 1)), (cotangent, (0, 1)), (tiles, (1, 2))))
    row_shift, output_tile_index, field, cotangent, tiles, mix, w_in, w_out = (
        pltpu.with_memory_space_constraint(a, pltpu.HBM)
        for a in (row_shift, output_tile_index, field, cotangent, tiles, mix, w_in, w_out))
    out, gfield, total = pl.pallas_call(
        kernel,
        name="block",
        out_shape=(
            jax.ShapeDtypeStruct((ROWS, LON, D), BF16),
            jax.ShapeDtypeStruct((ROWS, LON, D), BF16),
            jax.ShapeDtypeStruct((TILES, 16, 128), BF16),
        ),
        in_specs=[smem, smem, anywhere, anywhere, vmem, anywhere, anywhere, anywhere],
        out_specs=[vmem] * 3,
        scratch_shapes=[
            v((LON, ROWS, D), BF16), v((LON, ROWS, D), BF16), v((K, G, DG, DG), BF16), v((D, HID), BF16), v((HID, D), BF16),
            dma((5,)),
            v((6, EXT, D), BF16), v((6, WH, D), BF16), v((2, WH, D), BF16), v((2, WH, D), BF16), v((WH, D), BF16), v((WH, D), BF16),
            v((ROWS * NJ, K * JB, D), F32), v((ROWS, PAD, D), BF16),
            v((32, 128), F32), v((ROWS, K * JB, OFF * WIN), BF16), v((K * D, D), BF16), v((CELLS, K * D), BF16),
            v((CELLS, D), BF16), v((CELLS, HID), BF16), v((CELLS, HID), BF16), v((CELLS, HID), F32), v((CELLS, 256), F32),
            v((CELLS, D), BF16), v((CELLS, K * D), BF16), v((6, EXT, D), F32),
            v((2, NJ * MID, D), BF16), v((2, NJ * MID, D), BF16), v((2, 2, WH, D), BF16), v((2, 2, WH, D), BF16),
            v((WH, D), BF16), v((WH, D), BF16), v((2, PAD, D), BF16), v((2, PAD, D), BF16),
            v((2, 6, WH, D), BF16), v((2, 6, WH, D), BF16),
            v((TILES, 16, 128), BF16), v((2, HALF, 16, 128), BF16), v((2, HALF, 16, 128), BF16),
            v((2, 16, PER, 16, 128), BF16), v((2, PER, 16, 128), F32), v((2, PER, 16, 128), BF16),
            v((2, 16, 16, 128), BF16), v((2, PER, 16, 128), BF16),
            dma((13,)), dma((13,)), dma((13,)), dma((13,)), dma((2,)), dma((2,)),
        ] + [dma((2, 16))] * 10,
        compiler_params=pltpu.CompilerParams(collective_id=0, has_side_effects=True, vmem_limit_bytes=48 * 2**20),
        cost_estimate=pl.CostEstimate(flops=4 * 10**9, bytes_accessed=8 * 10**6, transcendentals=3 * 10**5),
    )(row_shift, output_tile_index, field, cotangent, tiles, mix, w_in, w_out)
    out, gfield, gmix, gin, gout = pl.pallas_call(
        unpack,
        name="unpack",
        out_shape=(
            jax.ShapeDtypeStruct((LON, ROWS, D), BF16),
            jax.ShapeDtypeStruct((LON, ROWS, D), BF16),
            jax.ShapeDtypeStruct((K, G, DG, DG), BF16),
            jax.ShapeDtypeStruct((D, HID), BF16),
            jax.ShapeDtypeStruct((HID, D), BF16),
        ),
        in_specs=[vmem] * 3,
        out_specs=[vmem] * 5,
        compiler_params=pltpu.CompilerParams(vmem_limit_bytes=48 * 2**20),
    )(total, out, gfield)
    return jnp.swapaxes(out, 0, 1), jnp.swapaxes(gfield, 0, 1), gmix, gin, gout


def solution(mesh):
    grid = P("lat", "lon", None)
    return jax.shard_map(
        body,
        mesh=mesh,
        in_specs=(grid, P("lat"), P("lat"), P(), P(), P(), P(), grid),
        out_specs=(grid, grid, P(), P(), P()),
        check_vma=False,
    )
```
